512 devices in a mesh: tok: 64 (over y, z), feat: 8 (over x, core).
Axes of the slice: x: 4, y: 4, z: 16, core: 2. Of those that a mesh axis runs over, the one named last changes fastest.
Arguments:
- activations: bfloat16 [131072, 8192], P('tok', 'feat'), may hold values from -16 to 16
- targets: bfloat16 [131072, 512], P('tok', 'feat'), may hold values from -6 to 6
Outputs:
- gram_block: float32 [8192, 512], P(('feat', 'tok'))
- cross_block: float32 [8192, 512], P(('feat', 'tok'))
The draws below stay inside these ranges and needn't reach their ends.
All inputs are finite; a program needn't handle non-finite values.
Results may differ from the reference program's by a relative error of at most 0.0003.
Values may be sent and summed in bfloat16 or wider, within the bound.
A program may use at most 64 MiB of HBM per device.

```python
import jax
import jax.numpy as jnp
from jax import lax

D = 8192
COLS = 512
TOKENS = 131072
PANEL = 1024
CW = 64


def with_spikes(values, rng, source, target, parts, factor):
    def block_of(position):
        return (jnp.arange(values.shape[position]) // (values.shape[position] // parts)).reshape((-1,) + (1,) * (values.ndim - 1 - position))

    near = jax.random.permutation(rng, parts)[block_of(target)]
    second = (block_of(target) + parts // 2) % parts
    return jnp.where((block_of(source) == near) | (block_of(source) == second), factor * values, values)


def levels(stream_key, shape, cuts, least, high):
    gain, own = 1.0, jax.random.fold_in(stream_key, 6)
    for dim, blocks in cuts:
        heights = jnp.exp(jax.random.uniform(jax.random.fold_in(own, dim), (blocks,), jnp.float32, least / len(cuts), high / len(cuts)))
        gain = gain * jnp.repeat(heights, shape[dim] // blocks).reshape([-1 if axis == dim else 1 for axis in range(len(shape))])
    return gain


def noise(stream_key, shape, spread, reach, shards=(), dtype=jnp.bfloat16):
    entries = spread * jax.random.normal(stream_key, shape, jnp.float32)
    if shards:
        entries = entries * levels(stream_key, shape, shards, -0.22, 0.18)
    return jnp.clip(entries, -reach, reach).astype(dtype)


def bell_draw_with(rng, shape, deviation, most, cuts, heavy, kind=jnp.bfloat16):
    array = deviation * jax.random.normal(rng, shape, jnp.float32)
    if cuts:
        array = array * levels(rng, shape, cuts, -0.22, 0.18)
    return jnp.clip(with_spikes(array, jax.random.fold_in(rng, 3), *heavy), -most, most).astype(kind)


def setup_inputs(seed: int = 0) -> dict:
    seeds = jax.random.split(jax.random.key(seed), 3)
    activations = bell_draw_with(seeds[0], (TOKENS, D), 1.0, 16.0, ((0, 64), (1, 8)), (0, 1, 64, 4.0))
    targets = noise(seeds[1], (TOKENS, COLS), 1.0, 6.0, ((0, 64), (1, 8)))
    return dict(activations=activations, targets=targets)


def reference(activations, targets):
    panels = D // PANEL
    window = activations.reshape(TOKENS, panels, PANEL)[:, :, :CW].reshape(TOKENS, COLS)
    dims = (((0,), (0,)), ((), ()))
    gram_block = lax.dot_general(activations, window, dims, preferred_element_type=jnp.float32)
    cross_block = lax.dot_general(activations, targets, dims, preferred_element_type=jnp.float32)
    return gram_block, cross_block
```

```python
import functools

import jax
import jax.numpy as jnp
from jax import lax
from jax.experimental import pallas as pl
from jax.experimental.pallas import tpu as pltpu
from jax.sharding import PartitionSpec as P

MESH = pl.DeviceIdType.MESH
NX, NY, ZH, ZL = 4, 4, 4, 4
OWN, LEFT, RIGHT, OPP = range(4)
PAD = 16
POWER, TOP = 12, 10.5


def packed(values):
    most = jnp.max(jnp.abs(values), axis=(0, 1), keepdims=True)
    scale = jnp.floor(TOP - jnp.log2(jnp.maximum(most, 1e-30)))
    x = values * jnp.exp2(scale)
    x2 = x * x
    x4 = x2 * x2
    code = x4 * x4 * x4
    code = jnp.where(x < 0, -code, code).astype(jnp.bfloat16)
    return code, jnp.broadcast_to(scale, (PAD, values.shape[1])).astype(jnp.bfloat16)


def unpacked(ref, rows):
    scale = ref[pl.ds(rows, PAD), :].astype(jnp.float32)[0:1]
    code = ref[pl.ds(0, rows), :].astype(jnp.float32)
    size = jnp.exp2(jnp.log2(jnp.maximum(jnp.abs(code), 1e-37)) * (1.0 / POWER) - scale)
    return jnp.where(code > 0, size, jnp.where(code < 0, -size, 0.0))


def kernel(
    sizes, a_hbm, t_hbm, gram_ref, cross_ref,
    a_ref, t_ref, at_ref, g_ref, ysend, yrecv, yown, ysum, asend, arecv, asum, brecv,
    in_sem, gs_sem, gr_sem, cs_sem, cr_sem, ys_sem, yr_sem, as_sem, ar_sem, bs_sem, br_sem,
):
    nx, ny, zh, zl = sizes
    tok, feat = lax.axis_index("tok"), lax.axis_index("feat")
    x, core = feat // 2, lax.rem(feat, 2)
    y, z = tok // (zh * zl), lax.rem(tok, zh * zl)
    h, l = z // zl, lax.rem(z, zl)
    tokens, feats = a_ref.shape
    half = tokens // 2
    width = t_ref.shape[1]
    yrows, arows, brows = feats // ny, feats // (ny * zl), feats // (ny * zl * zh)

    def at(dx=0, other=False, dy=0, dl=0, dh=0):
        xx = lax.rem(x + dx + nx, nx)
        cc = 1 - core if other else core
        yy = lax.rem(y + dy, ny)
        zz = lax.rem(h + dh, zh) * zl + lax.rem(l + dl, zl)
        return {"tok": yy * (zh * zl) + zz, "feat": xx * 2 + cc}

    first = pltpu.make_async_copy(a_hbm.at[:, pl.ds(0, 2 * width)], a_ref.at[:, pl.ds(0, 2 * width)], in_sem.at[0])
    mine = pltpu.make_async_copy(t_hbm, t_ref, in_sem.at[1])
    rest = pltpu.make_async_copy(
        a_hbm.at[:, pl.ds(2 * width, feats - 2 * width)],
        a_ref.at[:, pl.ds(2 * width, feats - 2 * width)], in_sem.at[2])
    first.start()
    mine.start()
    rest.start()

    peers = [at(other=True), at(dx=1), at(dx=-1)]
    peers += [at(dy=k) for k in range(1, ny)]
    peers += [at(dl=k) for k in range(1, zl)]
    peers += [at(dh=k) for k in range(1, zh)]
    barrier = pltpu.get_barrier_semaphore()
    for peer in peers:
        pl.semaphore_signal(barrier, inc=1, device_id=peer, device_id_type=MESH)
    pl.semaphore_wait(barrier, len(peers))

    first.wait()
    mine.wait()
    own = g_ref.at[OWN, core]
    own[:, pl.ds(0, width)] = a_ref[:, pl.ds(0, width)]
    own[:, pl.ds(width, width)] = t_ref[...]

    def remote(src, dst, send, recv, peer):
        return pltpu.make_async_remote_copy(
            src_ref=src, dst_ref=dst, send_sem=send, recv_sem=recv, device_id=peer, device_id_type=MESH)

    def rows(part):
        return pl.ds(part * half, half)

    def hop(part, direction):
        slot = LEFT if direction > 0 else RIGHT
        return remote(own.at[rows(part)], g_ref.at[slot, core, rows(part)],
                      gs_sem.at[slot, part], gr_sem.at[slot, part], at(dx=direction))

    def forward(part):
        slot, direction = (LEFT, 1) if part == 0 else (RIGHT, -1)
        return remote(g_ref.at[slot, core, rows(part)], g_ref.at[OPP, core, rows(part)],
                      gs_sem.at[OPP, part], gr_sem.at[OPP, part], at(dx=direction))

    def across(slot, part):
        block = g_ref.at[slot, core, rows(part)]
        return remote(block, block, cs_sem.at[slot, part], cr_sem.at[slot, part], at(other=True))

    def crossed(slot, part):
        block = g_ref.at[slot, 1 - core, rows(part)]
        return remote(block, block, cs_sem.at[slot, part], cr_sem.at[slot, part], at(other=True))

    hops = {(0, 1): hop(0, 1), (1, -1): hop(1, -1), (1, 1): hop(1, 1), (0, -1): hop(0, -1)}
    for copy in hops.values():
        copy.start()
    sent = list(hops.values())
    for part in range(2):
        copy = across(OWN, part)
        copy.start()
        sent.append(copy)

    rest.wait()
    tile = 128

    def transpose(i, carry):
        columns = pl.ds(pl.multiple_of(i * tile, tile), tile)
        at_ref[columns, :] = a_ref[:, columns].T
        return carry

    lax.fori_loop(0, feats // tile, transpose, 0)

    def term(stage, yy):
        block = at_ref[pl.ds(pl.multiple_of(yy * yrows, yrows), yrows), :]
        both = jnp.concatenate([g_ref[stage, 0], g_ref[stage, 1]], axis=1)
        return jnp.dot(block, both, preferred_element_type=jnp.float32)

    def ycopy(stage, k):
        return remote(ysend.at[stage, k - 1], yrecv.at[stage, k - 1],
                      ys_sem.at[stage, k - 1], yr_sem.at[stage, k - 1], at(dy=k))

    def multiply(stage):
        def step(k, carry):
            scaled, exponent = packed(term(stage, lax.rem(y + k, ny)))
            ysend[stage, k - 1, pl.ds(0, yrows), :] = scaled
            ysend[stage, k - 1, pl.ds(yrows, PAD), :] = exponent
            ycopy(stage, k).start()
            return carry

        lax.fori_loop(1, ny, step, 0)
        yown[stage] = term(stage, y)

    def acopy(stage, k):
        return remote(asend.at[stage, k - 1], arecv.at[stage, k - 1],
                      as_sem.at[stage, k - 1], ar_sem.at[stage, k - 1], at(dl=k))

    def slots(ll):
        return jnp.concatenate(
            [ysum[pl.ds(pl.multiple_of((g * zl + ll) * brows, brows), brows), :] for g in range(zh)], axis=0)

    def sum_y(stage):
        total = yown[stage]
        for k in range(1, ny):
            ycopy(stage, k).wait_recv()
            total += unpacked(yrecv.at[stage, k - 1], yrows)
        ysum[...] = total
        for k in range(1, zl):
            scaled, exponent = packed(slots(lax.rem(l + k, zl)))
            asend[stage, k - 1, pl.ds(0, arows), :] = scaled
            asend[stage, k - 1, pl.ds(arows, PAD), :] = exponent
            acopy(stage, k).start()
        asum[stage] = slots(l)

    def bcopy(stage, k):
        there = pl.ds(pl.multiple_of(lax.rem(h + k, zh) * brows, brows), brows)
        return remote(asum.at[stage, there], brecv.at[stage, k - 1],
                      bs_sem.at[stage, k - 1], br_sem.at[stage, k - 1], at(dh=k))

    def sum_a(stage):
        total = asum[stage]
        for k in range(1, zl):
            acopy(stage, k).wait_recv()
            total += unpacked(arecv.at[stage, k - 1], arows)
        asum[stage] = total
        for k in range(1, zh):
            bcopy(stage, k).start()

    def sum_b(stage):
        total = asum[stage, pl.ds(pl.multiple_of(h * brows, brows), brows), :]
        for k in range(1, zh):
            bcopy(stage, k).wait_recv()
            total += brecv[stage, k - 1]
        chip = lax.rem(x + {OWN: 0, LEFT: nx - 1, RIGHT: 1, OPP: 2}[stage], nx)
        columns = pl.ds(pl.multiple_of(chip * 2 * width, 2 * width), 2 * width)
        pieces = [total[:, i * width : (i + 1) * width] for i in range(4)]
        gram_ref[:, columns] = jnp.concatenate([pieces[0], pieces[2]], axis=1)
        cross_ref[:, columns] = jnp.concatenate([pieces[1], pieces[3]], axis=1)

    def pass_on(slot, part):
        copy = across(slot, part)
        copy.start()
        sent.append(copy)

    def go_on(part):
        copy = forward(part)
        copy.start()
        sent.append(copy)

    def get(slot):
        for part in range(2):
            crossed(slot, part).wait_recv()

    get(OWN)
    multiply(OWN)
    hops[0, 1].wait_recv()
    go_on(0)
    pass_on(LEFT, 0)
    hops[1, -1].wait_recv()
    go_on(1)
    pass_on(RIGHT, 1)
    hops[1, 1].wait_recv()
    pass_on(LEFT, 1)
    hops[0, -1].wait_recv()
    pass_on(RIGHT, 0)
    sum_y(OWN)
    get(LEFT)
    multiply(LEFT)
    get(RIGHT)
    multiply(RIGHT)
    for part in range(2):
        forward(part).wait_recv()
        pass_on(OPP, part)
    sum_a(OWN)
    get(OPP)
    multiply(OPP)
    sum_y(LEFT)
    sum_b(OWN)
    sum_y(RIGHT)
    sum_a(LEFT)
    sum_y(OPP)
    sum_a(RIGHT)
    sum_b(LEFT)
    sum_a(OPP)
    sum_b(RIGHT)
    sum_b(OPP)

    for copy in sent:
        copy.wait_send()
    for stage in range(4):
        for k in range(1, ny):
            ycopy(stage, k).wait_send()
        for k in range(1, zl):
            acopy(stage, k).wait_send()
        for k in range(1, zh):
            bcopy(stage, k).wait_send()


def shards(sizes, activations, targets):
    nx, ny, zh, zl = sizes
    tokens, feats = activations.shape
    width = targets.shape[1]
    two = 4 * width
    yrows, arows, brows = feats // ny, feats // (ny * zl), feats // (ny * zl * zh)
    out = jax.ShapeDtypeStruct((brows, nx * 2 * width), jnp.float32)
    dma = pltpu.SemaphoreType.DMA
    return pl.pallas_call(
        functools.partial(kernel, sizes),
        out_shape=(out, out),
        in_specs=[pl.BlockSpec(memory_space=pl.ANY)] * 2,
        out_specs=(pl.BlockSpec(memory_space=pltpu.VMEM),) * 2,
        scratch_shapes=[
            pltpu.VMEM((tokens, feats), jnp.bfloat16),
            pltpu.VMEM((tokens, width), jnp.bfloat16),
            pltpu.VMEM((feats, tokens), jnp.bfloat16),
            pltpu.VMEM((4, 2, tokens, 2 * width), jnp.bfloat16),
            pltpu.VMEM((4, ny - 1, yrows + PAD, two), jnp.bfloat16),
            pltpu.VMEM((4, ny - 1, yrows + PAD, two), jnp.bfloat16),
            pltpu.VMEM((4, yrows, two), jnp.float32),
            pltpu.VMEM((yrows, two), jnp.float32),
            pltpu.VMEM((4, zl - 1, arows + PAD, two), jnp.bfloat16),
            pltpu.VMEM((4, zl - 1, arows + PAD, two), jnp.bfloat16),
            pltpu.VMEM((4, arows, two), jnp.float32),
            pltpu.VMEM((4, zh - 1, brows, two), jnp.float32),
            dma((3,)),
            dma((4, 2)), dma((4, 2)),
            dma((4, 2)), dma((4, 2)),
            dma((4, ny - 1)), dma((4, ny - 1)),
            dma((4, zl - 1)), dma((4, zl - 1)),
            dma((4, zh - 1)), dma((4, zh - 1)),
        ],
        compiler_params=pltpu.CompilerParams(
            collective_id=0, has_side_effects=True, vmem_limit_bytes=48 * 1024 * 1024),
        cost_estimate=pl.CostEstimate(
            flops=2 * tokens * feats * nx * 4 * width, bytes_accessed=2 * tokens * feats, transcendentals=0),
    )(activations, targets)


def solution(mesh, sizes=(NX, NY, ZH, ZL)):
    return jax.shard_map(
        functools.partial(shards, sizes),
        mesh=mesh,
        in_specs=(P("tok", "feat"), P("tok", "feat")),
        out_specs=(P(("feat", "tok"), None), P(("feat", "tok"), None)),
        check_vma=False,
    )
```

```python
import functools

import jax
import jax.numpy as jnp
from jax import lax
from jax.experimental import pallas as pl
from jax.experimental.pallas import tpu as pltpu
from jax.sharding import PartitionSpec as P

MESH = pl.DeviceIdType.MESH
NX, NY, ZH, ZL = 4, 4, 4, 4
OWN, LEFT, RIGHT, OPP = range(4)
STAGES = (((OWN, 0), (OWN, 1)), ((LEFT, 0), (RIGHT, 0)), ((LEFT, 1), (RIGHT, 1)), ((OPP, 0), (OPP, 1)))
PAD = 16
POWER, TOP = 12, 10.5


def packed(values):
    most = jnp.max(jnp.abs(values), axis=(0, 1), keepdims=True)
    scale = jnp.floor(TOP - jnp.log2(jnp.maximum(most, 1e-30)))
    x = values * jnp.exp2(scale)
    x2 = x * x
    x4 = x2 * x2
    code = x4 * x4 * x4
    code = jnp.where(x < 0, -code, code).astype(jnp.bfloat16)
    return code, jnp.broadcast_to(scale, (PAD, values.shape[1])).astype(jnp.bfloat16)


def unpacked(ref, rows):
    scale = ref[pl.ds(rows, PAD), :].astype(jnp.float32)[0:1]
    code = ref[pl.ds(0, rows), :].astype(jnp.float32)
    size = jnp.exp2(jnp.log2(jnp.maximum(jnp.abs(code), 1e-37)) * (1.0 / POWER) - scale)
    return jnp.where(code > 0, size, jnp.where(code < 0, -size, 0.0))


def kernel(
    sizes, a_hbm, t_hbm, gram_ref, cross_ref,
    a_ref, t_ref, at_ref, g_ref, ysend, yrecv, yown, ysum, asend, arecv, asum, brecv, fin,
    in_sem, gs_sem, gr_sem, fs_sem, fr_sem, cs_sem, cr_sem, ys_sem, yr_sem, as_sem, ar_sem, bs_sem, br_sem,
    near_sem, far_sem,
):
    nx, ny, zh, zl = sizes
    tok, feat = lax.axis_index("tok"), lax.axis_index("feat")
    x, core = feat // 2, lax.rem(feat, 2)
    y, z = tok // (zh * zl), lax.rem(tok, zh * zl)
    h, l = z // zl, lax.rem(z, zl)
    tokens, feats = a_ref.shape
    half, quarter = tokens // 2, tokens // 4
    width = t_ref.shape[0]
    yrows, arows, brows = feats // ny, feats // (ny * zl), feats // (ny * zl * zh)

    def at(dx=0, dy=0, dl=0, dh=0, on=core):
        xx = lax.rem(x + dx + nx, nx)
        yy = lax.rem(y + dy, ny)
        zz = lax.rem(h + dh, zh) * zl + lax.rem(l + dl, zl)
        return {"tok": yy * (zh * zl) + zz, "feat": xx * 2 + on}

    partner = at(on=1 - core)
    first = pltpu.make_async_copy(a_hbm.at[:, pl.ds(0, 2 * width)], a_ref.at[:, pl.ds(0, 2 * width)], in_sem.at[0])
    mine = pltpu.make_async_copy(t_hbm, t_ref, in_sem.at[1])
    rest = pltpu.make_async_copy(
        a_hbm.at[:, pl.ds(2 * width, feats - 2 * width)],
        a_ref.at[:, pl.ds(2 * width, feats - 2 * width)], in_sem.at[2])
    first.start()
    mine.start()
    rest.start()

    barrier = pltpu.get_barrier_semaphore()
    near = [dict(dx=1), dict(dx=-1)] + [dict(dy=k) for k in range(1, ny)]
    far = [dict(dl=k) for k in range(1, zl)] + [dict(dh=k) for k in range(1, zh)]
    for there in near:
        pl.semaphore_signal(barrier, inc=1, device_id=at(on=1, **there), device_id_type=MESH)
    for there in far:
        pl.semaphore_signal(barrier, inc=1, device_id=at(on=0, **there), device_id_type=MESH)

    @pl.when(core == 0)
    def _():
        pl.semaphore_signal(barrier, inc=1, device_id=partner, device_id_type=MESH)

    @pl.when(core == 1)
    def _():
        pl.semaphore_wait(barrier, 2 * len(near) + 1)
        pl.semaphore_signal(near_sem, inc=1, device_id=partner, device_id_type=MESH)

    @pl.when(core == 0)
    def _():
        pl.semaphore_wait(near_sem, 1)

    def meet_far():
        @pl.when(core == 0)
        def _():
            pl.semaphore_wait(barrier, 2 * len(far))
            pl.semaphore_signal(far_sem, inc=1, device_id=partner, device_id_type=MESH)

        @pl.when(core == 1)
        def _():
            pl.semaphore_wait(far_sem, 1)

    first.wait()
    mine.wait()
    own = g_ref.at[OWN, core]
    own[:, pl.ds(0, width)] = a_ref[:, pl.ds(0, width)]
    own[:, pl.ds(width, width)] = t_ref[...].T

    def remote(src, dst, send, recv, peer):
        return pltpu.make_async_remote_copy(
            src_ref=src, dst_ref=dst, send_sem=send, recv_sem=recv, device_id=peer, device_id_type=MESH)

    def rows(part):
        return pl.ds(pl.multiple_of(part * half, half), half)

    def rows4(part, q):
        return pl.ds(pl.multiple_of(part * half + q * quarter, quarter), quarter)

    def hop(slot, b):
        return remote(g_ref.at[OWN, b, rows(core)], g_ref.at[slot, b, rows(core)],
                      gs_sem.at[slot - 1, b], gr_sem.at[slot - 1, b], at(dx=1 if slot == LEFT else -1))

    def forward(slot, b):
        part = rows4(core, slot - 1)
        return remote(g_ref.at[slot, b, part], g_ref.at[OPP, b, part],
                      fs_sem.at[slot - 1, b], fr_sem.at[slot - 1, b], at(dx=1 if slot == LEFT else -1))

    def share(part):
        block = g_ref.at[OWN, core, rows(part)]
        return remote(block, block, cs_sem.at[OWN, part], cr_sem.at[OWN, part], partner)

    def shared(part):
        block = g_ref.at[OWN, 1 - core, rows(part)]
        return remote(block, block, cs_sem.at[OWN, part], cr_sem.at[OWN, part], partner)

    def across(slot, b):
        block = g_ref.at[slot, b, rows(core)]
        return remote(block, block, cs_sem.at[slot, b], cr_sem.at[slot, b], partner)

    def crossed(slot, b):
        block = g_ref.at[slot, b, rows(1 - core)]
        return remote(block, block, cs_sem.at[slot, b], cr_sem.at[slot, b], partner)

    share(1 - core).start()
    share(core).start()

    @pl.when(core == 0)
    def _():
        hop(LEFT, 0).start()
        hop(RIGHT, 0).start()

    shared(core).wait_recv()

    @pl.when(core == 1)
    def _():
        hop(LEFT, 0).start()
        hop(RIGHT, 0).start()

    hop(LEFT, 1).start()
    hop(RIGHT, 1).start()

    rest.wait()
    tile = 128

    def transpose(i, carry):
        columns = pl.ds(pl.multiple_of(i * tile, tile), tile)
        at_ref[columns, :] = a_ref[:, columns].T
        return carry

    lax.fori_loop(0, feats // tile, transpose, 0)

    def term(stage, yy):
        block = at_ref[pl.ds(pl.multiple_of(yy * yrows, yrows), yrows), :]
        both = jnp.concatenate([g_ref[slot, b] for slot, b in STAGES[stage]], axis=1)
        return jnp.dot(block, both, preferred_element_type=jnp.float32)

    def ycopy(stage, k):
        return remote(ysend.at[stage, k - 1], yrecv.at[stage, k - 1],
                      ys_sem.at[stage, k - 1], yr_sem.at[stage, k - 1], at(dy=k))

    def multiply(stage):
        def step(k, carry):
            scaled, exponent = packed(term(stage, lax.rem(y + k, ny)))
            ysend[stage, k - 1, pl.ds(0, yrows), :] = scaled
            ysend[stage, k - 1, pl.ds(yrows, PAD), :] = exponent
            ycopy(stage, k).start()
            return carry

        lax.fori_loop(1, ny, step, 0)
        yown[stage] = term(stage, y)

    def acopy(stage, k):
        return remote(asend.at[stage, k - 1], arecv.at[stage, k - 1],
                      as_sem.at[stage, k - 1], ar_sem.at[stage, k - 1], at(dl=k))

    def slots(ll):
        return jnp.concatenate(
            [ysum[pl.ds(pl.multiple_of((g * zl + ll) * brows, brows), brows), :] for g in range(zh)], axis=0)

    def sum_y(stage):
        total = yown[stage]
        for k in range(1, ny):
            ycopy(stage, k).wait_recv()
            total += unpacked(yrecv.at[stage, k - 1], yrows)
        ysum[...] = total
        if stage == 0:
            meet_far()
        for k in range(1, zl):
            scaled, exponent = packed(slots(lax.rem(l + k, zl)))
            asend[stage, k - 1, pl.ds(0, arows), :] = scaled
            asend[stage, k - 1, pl.ds(arows, PAD), :] = exponent
            acopy(stage, k).start()
        asum[stage] = slots(l)

    def bcopy(stage, k):
        there = pl.ds(pl.multiple_of(lax.rem(h + k, zh) * brows, brows), brows)
        return remote(asum.at[stage, there], brecv.at[stage, k - 1],
                      bs_sem.at[stage, k - 1], br_sem.at[stage, k - 1], at(dh=k))

    def sum_a(stage):
        total = asum[stage]
        for k in range(1, zl):
            acopy(stage, k).wait_recv()
            total += unpacked(arecv.at[stage, k - 1], arows)
        asum[stage] = total
        for k in range(1, zh):
            bcopy(stage, k).start()

    def sum_b(stage):
        total = asum[stage, pl.ds(pl.multiple_of(h * brows, brows), brows), :]
        for k in range(1, zh):
            bcopy(stage, k).wait_recv()
            total += brecv[stage, k - 1]
        fin[stage] = total

    def finish(shift, places):
        chip = lax.rem(x + shift, nx)
        columns = pl.ds(pl.multiple_of(chip * 2 * width, 2 * width), 2 * width)
        for out, skip in ((gram_ref, 0), (cross_ref, width)):
            out[:, columns] = jnp.concatenate(
                [fin[stage][:, side * 2 * width + skip : side * 2 * width + skip + width] for stage, side in places],
                axis=1)

    def take(b):
        for slot in (LEFT, RIGHT):
            hop(slot, b).wait_recv()
            across(slot, b).start()
            forward(slot, b).start()

    shared(1 - core).wait_recv()
    multiply(0)
    take(0)
    for slot in (LEFT, RIGHT):
        crossed(slot, 0).wait_recv()
    multiply(1)
    sum_y(0)
    take(1)
    for slot in (LEFT, RIGHT):
        crossed(slot, 1).wait_recv()
    multiply(2)
    sum_a(0)
    for b in range(2):
        for slot in (LEFT, RIGHT):
            forward(slot, b).wait_recv()
        across(OPP, b).start()
    sum_y(1)
    for b in range(2):
        crossed(OPP, b).wait_recv()
    multiply(3)
    sum_y(2)
    sum_a(1)
    sum_b(0)
    finish(0, ((0, 0), (0, 1)))
    sum_a(2)
    sum_y(3)
    sum_b(1)
    sum_b(2)
    finish(nx - 1, ((1, 0), (2, 0)))
    finish(1, ((1, 1), (2, 1)))
    sum_a(3)
    sum_b(3)
    finish(nx // 2, ((3, 0), (3, 1)))

    for part in range(2):
        share(part).wait_send()
    for b in range(2):
        for slot in (LEFT, RIGHT):
            hop(slot, b).wait_send()
            forward(slot, b).wait_send()
        for slot in (LEFT, RIGHT, OPP):
            across(slot, b).wait_send()
    for stage in range(4):
        for k in range(1, ny):
            ycopy(stage, k).wait_send()
        for k in range(1, zl):
            acopy(stage, k).wait_send()
        for k in range(1, zh):
            bcopy(stage, k).wait_send()


def shards(sizes, activations, targets):
    nx, ny, zh, zl = sizes
    tokens, feats = activations.shape
    width = targets.shape[1]
    two = 4 * width
    yrows, arows, brows = feats // ny, feats // (ny * zl), feats // (ny * zl * zh)
    out = jax.ShapeDtypeStruct((brows, nx * 2 * width), jnp.float32)
    dma = pltpu.SemaphoreType.DMA
    return pl.pallas_call(
        functools.partial(kernel, sizes),
        out_shape=(out, out),
        in_specs=[pl.BlockSpec(memory_space=pl.ANY)] * 2,
        out_specs=(pl.BlockSpec(memory_space=pltpu.VMEM),) * 2,
        scratch_shapes=[
            pltpu.VMEM((tokens, feats), jnp.bfloat16),
            pltpu.VMEM((width, tokens), jnp.bfloat16),
            pltpu.VMEM((feats, tokens), jnp.bfloat16),
            pltpu.VMEM((4, 2, tokens, 2 * width), jnp.bfloat16),
            pltpu.VMEM((4, ny - 1, yrows + PAD, two), jnp.bfloat16),
            pltpu.VMEM((4, ny - 1, yrows + PAD, two), jnp.bfloat16),
            pltpu.VMEM((4, yrows, two), jnp.float32),
            pltpu.VMEM((yrows, two), jnp.float32),
            pltpu.VMEM((4, zl - 1, arows + PAD, two), jnp.bfloat16),
            pltpu.VMEM((4, zl - 1, arows + PAD, two), jnp.bfloat16),
            pltpu.VMEM((4, arows, two), jnp.float32),
            pltpu.VMEM((4, zh - 1, brows, two), jnp.float32),
            pltpu.VMEM((4, brows, two), jnp.float32),
            dma((3,)),
            dma((2, 2)), dma((2, 2)),
            dma((2, 2)), dma((2, 2)),
            dma((4, 2)), dma((4, 2)),
            dma((4, ny - 1)), dma((4, ny - 1)),
            dma((4, zl - 1)), dma((4, zl - 1)),
            dma((4, zh - 1)), dma((4, zh - 1)),
            pltpu.SemaphoreType.REGULAR, pltpu.SemaphoreType.REGULAR,
        ],
        compiler_params=pltpu.CompilerParams(
            collective_id=0, has_side_effects=True, vmem_limit_bytes=60 * 1024 * 1024),
        cost_estimate=pl.CostEstimate(
            flops=2 * tokens * feats * nx * 4 * width, bytes_accessed=2 * tokens * feats, transcendentals=0),
    )(activations, targets.T)


def solution(mesh, sizes=(NX, NY, ZH, ZL)):
    return jax.shard_map(
        functools.partial(shards, sizes),
        mesh=mesh,
        in_specs=(P("tok", "feat"), P("tok", "feat")),
        out_specs=(P(("feat", "tok"), None), P(("feat", "tok"), None)),
        check_vma=False,
    )
```

```python
import functools

import jax
import jax.numpy as jnp
from jax import lax
from jax.experimental import pallas as pl
from jax.experimental.pallas import tpu as pltpu
from jax.sharding import PartitionSpec as P

MESH = pl.DeviceIdType.MESH
NX, NY, ZH, ZL = 4, 4, 4, 4
OWN, LEFT, RIGHT, OPP = range(4)
STAGES = (((OWN, 0), (OWN, 1)), ((LEFT, 0), (RIGHT, 0)), ((LEFT, 1), (RIGHT, 1)), ((OPP, 0), (OPP, 1)))
PIECES = ((0, 0, ZH), (1, 0, ZH), (2, 0, ZH // 2), (2, ZH // 2, ZH // 2), (3, 0, 1), (3, 1, 1), (3, 2, ZH - 2))
PAD = 16
POWER, TOP = 12, 10.5


def packed(values):
    most = jnp.max(jnp.abs(values), axis=(0, 1), keepdims=True)
    scale = jnp.floor(TOP - jnp.log2(jnp.maximum(most, 1e-30)))
    x = values * jnp.exp2(scale)
    x2 = x * x
    x4 = x2 * x2
    code = x4 * x4 * x4
    code = jnp.where(x < 0, -code, code).astype(jnp.bfloat16)
    return code, jnp.broadcast_to(scale, (PAD, values.shape[1])).astype(jnp.bfloat16)


def unpacked(ref, rows):
    scale = ref[pl.ds(rows, PAD), :].astype(jnp.float32)[0:1]
    code = ref[pl.ds(0, rows), :].astype(jnp.float32)
    size = jnp.exp2(jnp.log2(jnp.maximum(jnp.abs(code), 1e-37)) * (1.0 / POWER) - scale)
    return jnp.where(code > 0, size, jnp.where(code < 0, -size, 0.0))


def kernel(
    sizes, a_hbm, t_hbm, gram_ref, cross_ref,
    a_ref, t_ref, at_ref, g_ref, ysend, yrecv, yown, ysum, asend, arecv, asum, brecv, fin,
    in_sem, gs_sem, gr_sem, fs_sem, fr_sem, cs_sem, cr_sem, ys_sem, yr_sem, as_sem, ar_sem, bs_sem, br_sem,
    near_sem, far_sem,
):
    nx, ny, zh, zl = sizes
    tok, feat = lax.axis_index("tok"), lax.axis_index("feat")
    x, core = feat // 2, lax.rem(feat, 2)
    y, z = tok // (zh * zl), lax.rem(tok, zh * zl)
    h, l = z // zl, lax.rem(z, zl)
    tokens, feats = a_ref.shape
    half, quarter = tokens // 2, tokens // 4
    width = t_ref.shape[0]
    yrows, arows, brows = feats // ny, feats // (ny * zl), feats // (ny * zl * zh)

    def at(dx=0, dy=0, dl=0, dh=0, on=core):
        xx = lax.rem(x + dx + nx, nx)
        yy = lax.rem(y + dy, ny)
        zz = lax.rem(h + dh, zh) * zl + lax.rem(l + dl, zl)
        return {"tok": yy * (zh * zl) + zz, "feat": xx * 2 + on}

    partner = at(on=1 - core)
    first = pltpu.make_async_copy(a_hbm.at[:, pl.ds(0, 2 * width)], a_ref.at[:, pl.ds(0, 2 * width)], in_sem.at[0])
    mine = pltpu.make_async_copy(t_hbm, t_ref, in_sem.at[1])
    rest = pltpu.make_async_copy(
        a_hbm.at[:, pl.ds(2 * width, feats - 2 * width)],
        a_ref.at[:, pl.ds(2 * width, feats - 2 * width)], in_sem.at[2])
    first.start()
    mine.start()
    rest.start()

    barrier = pltpu.get_barrier_semaphore()
    near = [dict(dx=1), dict(dx=-1)] + [dict(dy=k) for k in range(1, ny)]
    far = [dict(dl=k) for k in range(1, zl)] + [dict(dh=k) for k in range(1, zh)]
    for there in near:
        pl.semaphore_signal(barrier, inc=1, device_id=at(on=1, **there), device_id_type=MESH)
    for there in far:
        pl.semaphore_signal(barrier, inc=1, device_id=at(on=0, **there), device_id_type=MESH)

    @pl.when(core == 0)
    def _():
        pl.semaphore_signal(barrier, inc=1, device_id=partner, device_id_type=MESH)

    @pl.when(core == 1)
    def _():
        pl.semaphore_wait(barrier, 2 * len(near) + 1)
        pl.semaphore_signal(near_sem, inc=1, device_id=partner, device_id_type=MESH)

    @pl.when(core == 0)
    def _():
        pl.semaphore_wait(near_sem, 1)

    def meet_far():
        @pl.when(core == 0)
        def _():
            pl.semaphore_wait(barrier, 2 * len(far))
            pl.semaphore_signal(far_sem, inc=1, device_id=partner, device_id_type=MESH)

        @pl.when(core == 1)
        def _():
            pl.semaphore_wait(far_sem, 1)

    first.wait()
    mine.wait()
    own = g_ref.at[OWN, core]
    own[:, pl.ds(0, width)] = a_ref[:, pl.ds(0, width)]
    own[:, pl.ds(width, width)] = t_ref[...].T

    def remote(src, dst, send, recv, peer):
        return pltpu.make_async_remote_copy(
            src_ref=src, dst_ref=dst, send_sem=send, recv_sem=recv, device_id=peer, device_id_type=MESH)

    def rows(part):
        return pl.ds(pl.multiple_of(part * half, half), half)

    def rows4(part, q):
        return pl.ds(pl.multiple_of(part * half + q * quarter, quarter), quarter)

    def hop(slot, b):
        return remote(g_ref.at[OWN, b, rows(core)], g_ref.at[slot, b, rows(core)],
                      gs_sem.at[slot - 1, b], gr_sem.at[slot - 1, b], at(dx=1 if slot == LEFT else -1))

    def forward(slot, b):
        part = rows4(core, slot - 1)
        return remote(g_ref.at[slot, b, part], g_ref.at[OPP, b, part],
                      fs_sem.at[slot - 1, b], fr_sem.at[slot - 1, b], at(dx=1 if slot == LEFT else -1))

    def share(part):
        block = g_ref.at[OWN, core, rows(part)]
        return remote(block, block, cs_sem.at[OWN, part], cr_sem.at[OWN, part], partner)

    def shared(part):
        block = g_ref.at[OWN, 1 - core, rows(part)]
        return remote(block, block, cs_sem.at[OWN, part], cr_sem.at[OWN, part], partner)

    def across(slot, b):
        block = g_ref.at[slot, b, rows(core)]
        return remote(block, block, cs_sem.at[slot, b], cr_sem.at[slot, b], partner)

    def crossed(slot, b):
        block = g_ref.at[slot, b, rows(1 - core)]
        return remote(block, block, cs_sem.at[slot, b], cr_sem.at[slot, b], partner)

    share(1 - core).start()
    share(core).start()

    @pl.when(core == 0)
    def _():
        hop(LEFT, 0).start()
        hop(RIGHT, 0).start()

    shared(core).wait_recv()

    @pl.when(core == 1)
    def _():
        hop(LEFT, 0).start()
        hop(RIGHT, 0).start()

    hop(LEFT, 1).start()
    hop(RIGHT, 1).start()

    rest.wait()
    tile = 128

    def transpose(i, carry):
        columns = pl.ds(pl.multiple_of(i * tile, tile), tile)
        at_ref[columns, :] = a_ref[:, columns].T
        return carry

    lax.fori_loop(0, feats // tile, transpose, 0)

    def ycopy(p, k):
        part = pl.ds(0, PIECES[p][2] * zl * brows + PAD)
        return remote(ysend.at[p, k - 1, part], yrecv.at[p, k - 1, part],
                      ys_sem.at[p, k - 1], yr_sem.at[p, k - 1], at(dy=k))

    def multiply(p):
        stage, low, count = PIECES[p]
        size = count * zl * brows
        both = jnp.concatenate([g_ref[slot, b] for slot, b in STAGES[stage]], axis=1)
        order = [2, 1, 3, 0] if ny == 4 else [*range(1, ny), 0]
        at_once = yrows // size
        for first_k in range(0, ny, at_once):
            group = order[first_k : first_k + at_once]
            block = jnp.concatenate(
                [at_ref[pl.ds(pl.multiple_of(lax.rem(y + k, ny) * yrows + low * zl * brows, zl * brows), size), :]
                 for k in group], axis=0)
            terms = jnp.dot(block, both, preferred_element_type=jnp.float32)
            for i, k in enumerate(group):
                term = terms[i * size : (i + 1) * size]
                if k == 0:
                    yown[p, pl.ds(0, size), :] = term
                    continue
                code, exponent = packed(term)
                ysend[p, k - 1, pl.ds(0, size), :] = code
                ysend[p, k - 1, pl.ds(size, PAD), :] = exponent
                ycopy(p, k).start()

    def acopy(p, k):
        part = pl.ds(0, PIECES[p][2] * brows + PAD)
        return remote(asend.at[p, k - 1, part], arecv.at[p, k - 1, part],
                      as_sem.at[p, k - 1], ar_sem.at[p, k - 1], at(dl=k))

    def slots(p, ll):
        return jnp.concatenate(
            [ysum[pl.ds(pl.multiple_of((g * zl + ll) * brows, brows), brows), :] for g in range(PIECES[p][2])], axis=0)

    def sum_y(p):
        size, asize = PIECES[p][2] * zl * brows, PIECES[p][2] * brows
        total = yown[p, pl.ds(0, size), :]
        for k in range(1, ny):
            ycopy(p, k).wait_recv()
            total += unpacked(yrecv.at[p, k - 1], size)
        ysum[pl.ds(0, size), :] = total
        if p == 0:
            meet_far()
        for k in range(1, zl):
            code, exponent = packed(slots(p, lax.rem(l + k, zl)))
            asend[p, k - 1, pl.ds(0, asize), :] = code
            asend[p, k - 1, pl.ds(asize, PAD), :] = exponent
            acopy(p, k).start()
        asum[p, pl.ds(0, asize), :] = slots(p, l)

    def inside(p, g):
        _, low, count = PIECES[p]
        return (g >= low) & (g < low + count)

    def bcopy(p, k):
        _, low, count = PIECES[p]
        there = lax.rem(lax.rem(h + k, zh) - low + zh, zh)
        if count == 1:
            there = 0
        part = pl.ds(pl.multiple_of(there * brows, brows), brows)
        return remote(asum.at[p, part], brecv.at[p, k - 1], bs_sem.at[p, k - 1], br_sem.at[p, k - 1], at(dh=k))

    def brecvd(p, k):
        part = pl.ds(0, brows)
        return remote(asum.at[p, part], brecv.at[p, k - 1], bs_sem.at[p, k - 1], br_sem.at[p, k - 1], at(dh=k))

    def sum_a(p):
        asize = PIECES[p][2] * brows
        total = asum[p, pl.ds(0, asize), :]
        for k in range(1, zl):
            acopy(p, k).wait_recv()
            total += unpacked(arecv.at[p, k - 1], asize)
        asum[p, pl.ds(0, asize), :] = total
        for k in range(1, zh):
            @pl.when(inside(p, lax.rem(h + k, zh)))
            def _():
                bcopy(p, k).start()

    def sum_b(p):
        stage, low, count = PIECES[p]

        @pl.when(inside(p, h))
        def _():
            mine = lax.rem(h - low + zh, zh) if count > 1 else 0
            total = asum[p, pl.ds(pl.multiple_of(mine * brows, brows), brows), :]
            for k in range(1, zh):
                brecvd(p, k).wait_recv()
                total += brecv[p, k - 1]
            fin[stage] = total

    def sent_b(p):
        for k in range(1, zh):
            @pl.when(inside(p, lax.rem(h + k, zh)))
            def _():
                brecvd(p, k).wait_send()

    def finish(shift, places):
        chip = lax.rem(x + shift, nx)
        columns = pl.ds(pl.multiple_of(chip * 2 * width, 2 * width), 2 * width)
        for out, skip in ((gram_ref, 0), (cross_ref, width)):
            out[:, columns] = jnp.concatenate(
                [fin[stage][:, side * 2 * width + skip : side * 2 * width + skip + width] for stage, side in places],
                axis=1)

    def take(b):
        for slot in (LEFT, RIGHT):
            hop(slot, b).wait_recv()
            across(slot, b).start()
            forward(slot, b).start()

    shared(1 - core).wait_recv()
    multiply(0)
    take(0)
    for slot in (LEFT, RIGHT):
        crossed(slot, 0).wait_recv()
    multiply(1)
    sum_y(0)
    take(1)
    for slot in (LEFT, RIGHT):
        crossed(slot, 1).wait_recv()
    multiply(2)
    multiply(3)
    sum_a(0)
    for b in range(2):
        for slot in (LEFT, RIGHT):
            forward(slot, b).wait_recv()
        across(OPP, b).start()
    sum_y(1)
    for b in range(2):
        crossed(OPP, b).wait_recv()
    multiply(4)
    multiply(5)
    multiply(6)
    sum_y(2)
    sum_a(1)
    sum_b(0)
    sum_y(3)
    sum_y(4)
    sum_a(2)
    sum_y(5)
    sum_a(3)
    sum_a(4)
    sum_y(6)
    sum_a(5)
    sum_b(1)
    finish(0, ((0, 0), (0, 1)))
    sum_a(6)
    sum_b(2)
    sum_b(3)
    finish(nx - 1, ((1, 0), (2, 0)))
    finish(1, ((1, 1), (2, 1)))
    sum_b(4)
    sum_b(5)
    sum_b(6)
    finish(nx // 2, ((3, 0), (3, 1)))

    for part in range(2):
        share(part).wait_send()
    for b in range(2):
        for slot in (LEFT, RIGHT):
            hop(slot, b).wait_send()
            forward(slot, b).wait_send()
        for slot in (LEFT, RIGHT, OPP):
            across(slot, b).wait_send()
    for p in range(len(PIECES)):
        for k in range(1, ny):
            ycopy(p, k).wait_send()
        for k in range(1, zl):
            acopy(p, k).wait_send()
        sent_b(p)


def shards(sizes, activations, targets):
    nx, ny, zh, zl = sizes
    tokens, feats = activations.shape
    width = targets.shape[1]
    two, n = 4 * width, len(PIECES)
    yrows, arows, brows = feats // ny, feats // (ny * zl), feats // (ny * zl * zh)
    out = jax.ShapeDtypeStruct((brows, nx * 2 * width), jnp.float32)
    dma = pltpu.SemaphoreType.DMA
    return pl.pallas_call(
        functools.partial(kernel, sizes),
        out_shape=(out, out),
        in_specs=[pl.BlockSpec(memory_space=pl.ANY)] * 2,
        out_specs=(pl.BlockSpec(memory_space=pltpu.VMEM),) * 2,
        scratch_shapes=[
            pltpu.VMEM((tokens, feats), jnp.bfloat16),
            pltpu.VMEM((width, tokens), jnp.bfloat16),
            pltpu.VMEM((feats, tokens), jnp.bfloat16),
            pltpu.VMEM((4, 2, tokens, 2 * width), jnp.bfloat16),
            pltpu.VMEM((n, ny - 1, yrows + PAD, two), jnp.bfloat16),
            pltpu.VMEM((n, ny - 1, yrows + PAD, two), jnp.bfloat16),
            pltpu.VMEM((n, yrows, two), jnp.float32),
            pltpu.VMEM((yrows, two), jnp.float32),
            pltpu.VMEM((n, zl - 1, arows + PAD, two), jnp.bfloat16),
            pltpu.VMEM((n, zl - 1, arows + PAD, two), jnp.bfloat16),
            pltpu.VMEM((n, arows, two), jnp.float32),
            pltpu.VMEM((n, zh - 1, brows, two), jnp.float32),
            pltpu.VMEM((4, brows, two), jnp.float32),
            dma((3,)),
            dma((2, 2)), dma((2, 2)),
            dma((2, 2)), dma((2, 2)),
            dma((4, 2)), dma((4, 2)),
            dma((n, ny - 1)), dma((n, ny - 1)),
            dma((n, zl - 1)), dma((n, zl - 1)),
            dma((n, zh - 1)), dma((n, zh - 1)),
            pltpu.SemaphoreType.REGULAR, pltpu.SemaphoreType.REGULAR,
        ],
        compiler_params=pltpu.CompilerParams(
            collective_id=0, has_side_effects=True, vmem_limit_bytes=53 * 1024 * 1024),
        cost_estimate=pl.CostEstimate(
            flops=2 * tokens * feats * nx * 4 * width, bytes_accessed=2 * tokens * feats, transcendentals=0),
    )(activations, targets.T)


def solution(mesh, sizes=(NX, NY, ZH, ZL)):
    return jax.shard_map(
        functools.partial(shards, sizes),
        mesh=mesh,
        in_specs=(P("tok", "feat"), P("tok", "feat")),
        out_specs=(P(("feat", "tok"), None), P(("feat", "tok"), None)),
        check_vma=False,
    )
```

```python
import functools

import jax
import jax.numpy as jnp
from jax import lax
from jax.experimental import pallas as pl
from jax.experimental.pallas import tpu as pltpu
from jax.sharding import PartitionSpec as P

MESH = pl.DeviceIdType.MESH
NX, NY, ZH, ZL = 4, 4, 4, 4
OWN, LEFT, RIGHT, OPP = range(4)
STAGES = (((OWN, 0), (OWN, 1)), ((LEFT, 0), (RIGHT, 0)), ((LEFT, 1), (RIGHT, 1)), ((OPP, 0), (OPP, 1)))
PIECES = ((0, 0, ZH), (1, 0, ZH), (2, 0, ZH // 2), (2, ZH // 2, ZH // 2), (3, 0, 1), (3, 1, 1), (3, 2, ZH - 2))
LANES = 128
POWER, TOP = 12, 10.5


def packed(values):
    most = jnp.max(jnp.abs(values), axis=(0, 1), keepdims=True)
    scale = jnp.floor(TOP - jnp.log2(jnp.maximum(most, 1e-30)))
    x = values * jnp.exp2(scale)
    x2 = x * x
    x4 = x2 * x2
    code = x4 * x4 * x4
    code = jnp.where(x < 0, -code, code).astype(jnp.bfloat16)
    return code, jnp.broadcast_to(scale, (1, LANES))


def unpacked(code, scale):
    code = code.astype(jnp.float32)
    scale = jnp.concatenate([scale] * (code.shape[1] // LANES), axis=1)
    size = jnp.exp2(jnp.log2(jnp.maximum(jnp.abs(code), 1e-37)) * (1.0 / POWER) - scale)
    return jnp.where(code > 0, size, jnp.where(code < 0, -size, 0.0))


def kernel(
    sizes, a_hbm, t_hbm, gram_ref, cross_ref,
    a_ref, t_ref, at_ref, g_ref, ysend, yrecv, yown, asend, arecv, aown, bsend, brecv, bown, fin,
    yexp, yexps, aexp, aexps, bexp, bexps,
    in_sem, gs_sem, gr_sem, fs_sem, fr_sem, cs_sem, cr_sem, ys_sem, yr_sem, as_sem, ar_sem, bs_sem, br_sem,
    ye_sem, yf_sem, ae_sem, af_sem, be_sem, bf_sem, near_sem, far_sem,
):
    nx, ny, zh, zl = sizes
    tok, feat = lax.axis_index("tok"), lax.axis_index("feat")
    x, core = feat // 2, lax.rem(feat, 2)
    y, z = tok // (zh * zl), lax.rem(tok, zh * zl)
    shift = zl // 2 * core
    turned = lax.rem(z + shift, zh * zl)
    h, l = turned // zl, lax.rem(turned, zl)
    tokens, feats = a_ref.shape
    half, quarter = tokens // 2, tokens // 4
    width = t_ref.shape[0]
    yrows, arows, brows = feats // ny, feats // (ny * zl), feats // (ny * zl * zh)

    def at(dx=0, dy=0, dl=0, dh=0, on=core):
        xx = lax.rem(x + dx + nx, nx)
        yy = lax.rem(y + dy, ny)
        zz = lax.rem(h + dh, zh) * zl + lax.rem(l + dl, zl)
        zz = lax.rem(zz + zh * zl - shift, zh * zl)
        return {"tok": yy * (zh * zl) + zz, "feat": xx * 2 + on}

    partner = at(on=1 - core)
    first = pltpu.make_async_copy(a_hbm.at[:, pl.ds(0, 2 * width)], a_ref.at[:, pl.ds(0, 2 * width)], in_sem.at[0])
    mine = pltpu.make_async_copy(t_hbm, t_ref, in_sem.at[1])
    rest = pltpu.make_async_copy(
        a_hbm.at[:, pl.ds(2 * width, feats - 2 * width)],
        a_ref.at[:, pl.ds(2 * width, feats - 2 * width)], in_sem.at[2])
    first.start()
    mine.start()
    rest.start()

    barrier = pltpu.get_barrier_semaphore()
    near = [dict(dx=1), dict(dx=-1)] + [dict(dy=k) for k in range(1, ny)]
    far = [dict(dl=k) for k in range(1, zl)] + [dict(dh=k) for k in range(1, zh)]
    for there in near:
        pl.semaphore_signal(barrier, inc=1, device_id=at(on=1, **there), device_id_type=MESH)
    for there in far:
        pl.semaphore_signal(barrier, inc=1, device_id=at(on=0, **there), device_id_type=MESH)

    @pl.when(core == 0)
    def _():
        pl.semaphore_signal(barrier, inc=1, device_id=partner, device_id_type=MESH)

    first.wait()
    mine.wait()
    own = g_ref.at[OWN, core]
    own[:, pl.ds(0, width)] = a_ref[:, pl.ds(0, width)]
    own[:, pl.ds(width, width)] = t_ref[...].T

    @pl.when(core == 1)
    def _():
        pl.semaphore_wait(barrier, 2 * len(near) + 1)
        pl.semaphore_signal(near_sem, inc=1, device_id=partner, device_id_type=MESH)

    @pl.when(core == 0)
    def _():
        pl.semaphore_wait(near_sem, 1)

    def meet_far():
        @pl.when(core == 0)
        def _():
            pl.semaphore_wait(barrier, 2 * len(far))
            pl.semaphore_signal(far_sem, inc=1, device_id=partner, device_id_type=MESH)

        @pl.when(core == 1)
        def _():
            pl.semaphore_wait(far_sem, 1)

    def remote(src, dst, send, recv, peer):
        return pltpu.make_async_remote_copy(
            src_ref=src, dst_ref=dst, send_sem=send, recv_sem=recv, device_id=peer, device_id_type=MESH)

    def rows(part):
        return pl.ds(pl.multiple_of(part * half, half), half)

    def rows4(part, q):
        return pl.ds(pl.multiple_of(part * half + q * quarter, quarter), quarter)

    def hop(slot, b):
        return remote(g_ref.at[OWN, b, rows(core)], g_ref.at[slot, b, rows(core)],
                      gs_sem.at[slot - 1, b], gr_sem.at[slot - 1, b], at(dx=1 if slot == LEFT else -1))

    def forward(slot, b):
        part = rows4(core, slot - 1)
        return remote(g_ref.at[slot, b, part], g_ref.at[OPP, b, part],
                      fs_sem.at[slot - 1, b], fr_sem.at[slot - 1, b], at(dx=1 if slot == LEFT else -1))

    def share(part):
        block = g_ref.at[OWN, core, rows(part)]
        return remote(block, block, cs_sem.at[OWN, part], cr_sem.at[OWN, part], partner)

    def shared(part):
        block = g_ref.at[OWN, 1 - core, rows(part)]
        return remote(block, block, cs_sem.at[OWN, part], cr_sem.at[OWN, part], partner)

    def across(slot, b):
        block = g_ref.at[slot, b, rows(core)]
        return remote(block, block, cs_sem.at[slot, b], cr_sem.at[slot, b], partner)

    def crossed(slot, b):
        block = g_ref.at[slot, b, rows(1 - core)]
        return remote(block, block, cs_sem.at[slot, b], cr_sem.at[slot, b], partner)

    share(1 - core).start()
    share(core).start()

    @pl.when(core == 0)
    def _():
        hop(LEFT, 0).start()
        hop(RIGHT, 0).start()

    shared(core).wait_recv()

    @pl.when(core == 1)
    def _():
        hop(LEFT, 0).start()
        hop(RIGHT, 0).start()

    hop(LEFT, 1).start()
    hop(RIGHT, 1).start()

    rest.wait()
    tile = 128

    def transpose(i, carry):
        columns = pl.ds(pl.multiple_of(i * tile, tile), tile)
        at_ref[columns, :] = a_ref[:, columns].T
        return carry

    lax.fori_loop(0, feats // tile, transpose, 0)

    def ycopies(p, k):
        part = pl.ds(0, PIECES[p][2] * zl * brows)
        return (remote(ysend.at[p, k - 1, part], yrecv.at[p, k - 1, part],
                       ys_sem.at[p, k - 1], yr_sem.at[p, k - 1], at(dy=k)),
                remote(yexp.at[p * (ny - 1) + k - 1], yexps.at[p * (ny - 1) + k - 1],
                       ye_sem.at[p, k - 1], yf_sem.at[p, k - 1], at(dy=k)))

    def acopies(p, k):
        size = PIECES[p][2] * brows
        there = pl.ds(pl.multiple_of(lax.rem(l + k, zl) * size, brows), size)
        return (remote(asend.at[p, there], arecv.at[p, k - 1, pl.ds(0, size)],
                       as_sem.at[p, k - 1], ar_sem.at[p, k - 1], at(dl=k)),
                remote(aexp.at[p], aexps.at[p * (zl - 1) + k - 1],
                       ae_sem.at[p, k - 1], af_sem.at[p, k - 1], at(dl=k)))

    def bcopies(p, k):
        _, low, count = PIECES[p]
        place = lax.rem(lax.rem(h + k, zh) - low + zh, zh) if count > 1 else 0
        there = pl.ds(pl.multiple_of(lax.rem(place, count) * brows, brows), brows)
        return (remote(bsend.at[p, there], brecv.at[p, k - 1],
                       bs_sem.at[p, k - 1], br_sem.at[p, k - 1], at(dh=k)),
                remote(bexp.at[p], bexps.at[p * (zh - 1) + k - 1],
                       be_sem.at[p, k - 1], bf_sem.at[p, k - 1], at(dh=k)))

    def start(copies):
        for copy in copies:
            copy.start()

    def arrive(copies):
        for copy in copies:
            copy.wait_recv()

    def leave(copies):
        for copy in copies:
            copy.wait_send()

    def multiply(p):
        stage, low, count = PIECES[p]
        size = count * zl * brows
        both = jnp.concatenate([g_ref[slot, b] for slot, b in STAGES[stage]], axis=1)
        order = [2, 1, 3, 0] if ny == 4 else [*range(1, ny), 0]
        at_once = yrows // size
        for first_k in range(0, ny, at_once):
            group = order[first_k : first_k + at_once]
            parts = []
            for k in group:
                base = lax.rem(y + k, ny) * yrows
                for ll in range(zl):
                    for g in range(low, low + count):
                        owner = lax.rem(g * zl + ll + zh * zl - shift, zh * zl)
                        parts.append(at_ref[pl.ds(pl.multiple_of(base + owner * brows, brows), brows), :])
            terms = jnp.dot(jnp.concatenate(parts, axis=0), both, preferred_element_type=jnp.float32)
            for i, k in enumerate(group):
                term = terms[i * size : (i + 1) * size]
                if k == 0:
                    yown[p, pl.ds(0, size), :] = term
                    continue
                code, exponent = packed(term)
                ysend[p, k - 1, pl.ds(0, size), :] = code
                yexp[p * (ny - 1) + k - 1] = exponent
                start(ycopies(p, k))

    def sum_y(p):
        size, asize = PIECES[p][2] * zl * brows, PIECES[p][2] * brows
        total = yown[p, pl.ds(0, size), :]
        for k in range(1, ny):
            arrive(ycopies(p, k))
            total += unpacked(yrecv[p, k - 1, pl.ds(0, size), :], yexps[p * (ny - 1) + k - 1])
        code, exponent = packed(total)
        asend[p, pl.ds(0, size), :] = code
        aexp[p] = exponent
        if p == 0:
            meet_far()
        for k in range(1, zl):
            start(acopies(p, k))
        yown[p, pl.ds(0, size), :] = total
        aown[p, pl.ds(0, asize), :] = yown[p, pl.ds(pl.multiple_of(l * asize, brows), asize), :]

    def inside(p, g):
        _, low, count = PIECES[p]
        return (g >= low) & (g < low + count)

    def sum_a(p):
        asize = PIECES[p][2] * brows
        total = aown[p, pl.ds(0, asize), :]
        for k in range(1, zl):
            arrive(acopies(p, k))
            total += unpacked(arecv[p, k - 1, pl.ds(0, asize), :], aexps[p * (zl - 1) + k - 1])
        code, exponent = packed(total)
        bsend[p, pl.ds(0, asize), :] = code
        bexp[p] = exponent
        for k in range(1, zh):
            @pl.when(inside(p, lax.rem(h + k, zh)))
            def _():
                start(bcopies(p, k))
        bown[p, pl.ds(0, asize), :] = total

    def sum_b(p):
        stage, low, count = PIECES[p]

        @pl.when(inside(p, h))
        def _():
            mine = lax.rem(h - low + zh, zh) if count > 1 else 0
            total = bown[p, pl.ds(pl.multiple_of(lax.rem(mine, count) * brows, brows), brows), :]
            for k in range(1, zh):
                arrive(bcopies(p, k))
                total += unpacked(brecv[p, k - 1], bexps[p * (zh - 1) + k - 1])
            fin[stage] = total

    def sent_b(p):
        for k in range(1, zh):
            @pl.when(inside(p, lax.rem(h + k, zh)))
            def _():
                leave(bcopies(p, k))

    def finish(dx, places):
        chip = lax.rem(x + dx, nx)
        columns = pl.ds(pl.multiple_of(chip * 2 * width, 2 * width), 2 * width)
        for out, skip in ((gram_ref, 0), (cross_ref, width)):
            out[:, columns] = jnp.concatenate(
                [fin[stage][:, side * 2 * width + skip : side * 2 * width + skip + width] for stage, side in places],
                axis=1)

    def take(b):
        for slot in (LEFT, RIGHT):
            hop(slot, b).wait_recv()
            across(slot, b).start()
            forward(slot, b).start()

    shared(1 - core).wait_recv()
    multiply(0)
    take(0)
    for slot in (LEFT, RIGHT):
        crossed(slot, 0).wait_recv()
    multiply(1)
    sum_y(0)
    take(1)
    for slot in (LEFT, RIGHT):
        crossed(slot, 1).wait_recv()
    multiply(2)
    multiply(3)
    sum_a(0)
    for b in range(2):
        for slot in (LEFT, RIGHT):
            forward(slot, b).wait_recv()
        across(OPP, b).start()
    sum_y(1)
    for b in range(2):
        crossed(OPP, b).wait_recv()
    multiply(4)
    multiply(5)
    multiply(6)
    sum_y(2)
    sum_a(1)
    sum_y(3)
    sum_y(4)
    sum_a(2)
    sum_y(5)
    sum_a(3)
    sum_a(4)
    sum_y(6)
    sum_a(5)
    sum_b(0)
    finish(0, ((0, 0), (0, 1)))
    sum_a(6)
    sum_b(1)
    sum_b(2)
    sum_b(3)
    finish(nx - 1, ((1, 0), (2, 0)))
    finish(1, ((1, 1), (2, 1)))
    sum_b(4)
    sum_b(5)
    sum_b(6)
    finish(nx // 2, ((3, 0), (3, 1)))

    for part in range(2):
        share(part).wait_send()
    for b in range(2):
        for slot in (LEFT, RIGHT):
            hop(slot, b).wait_send()
            forward(slot, b).wait_send()
        for slot in (LEFT, RIGHT, OPP):
            across(slot, b).wait_send()
    for p in range(len(PIECES)):
        for k in range(1, ny):
            leave(ycopies(p, k))
        for k in range(1, zl):
            leave(acopies(p, k))
        sent_b(p)


def shards(sizes, activations, targets):
    nx, ny, zh, zl = sizes
    tokens, feats = activations.shape
    width = targets.shape[1]
    two, n = 4 * width, len(PIECES)
    yrows, arows, brows = feats // ny, feats // (ny * zl), feats // (ny * zl * zh)
    out = jax.ShapeDtypeStruct((brows, nx * 2 * width), jnp.float32)
    dma = pltpu.SemaphoreType.DMA
    return pl.pallas_call(
        functools.partial(kernel, sizes),
        out_shape=(out, out),
        in_specs=[pl.BlockSpec(memory_space=pl.ANY)] * 2,
        out_specs=(pl.BlockSpec(memory_space=pltpu.VMEM),) * 2,
        scratch_shapes=[
            pltpu.VMEM((tokens, feats), jnp.bfloat16),
            pltpu.VMEM((width, tokens), jnp.bfloat16),
            pltpu.VMEM((feats, tokens), jnp.bfloat16),
            pltpu.VMEM((4, 2, tokens, 2 * width), jnp.bfloat16),
            pltpu.VMEM((n, ny - 1, yrows, two), jnp.bfloat16),
            pltpu.VMEM((n, ny - 1, yrows, two), jnp.bfloat16),
            pltpu.VMEM((n, yrows, two), jnp.float32),
            pltpu.VMEM((n, yrows, two), jnp.bfloat16),
            pltpu.VMEM((n, zl - 1, arows, two), jnp.bfloat16),
            pltpu.VMEM((n, arows, two), jnp.float32),
            pltpu.VMEM((n, arows, two), jnp.bfloat16),
            pltpu.VMEM((n, zh - 1, brows, two), jnp.bfloat16),
            pltpu.VMEM((n, arows, two), jnp.float32),
            pltpu.VMEM((4, brows, two), jnp.float32),
            pltpu.VMEM((n * (ny - 1), 1, LANES), jnp.float32),
            pltpu.VMEM((n * (ny - 1), 1, LANES), jnp.float32),
            pltpu.VMEM((n, 1, LANES), jnp.float32),
            pltpu.VMEM((n * (zl - 1), 1, LANES), jnp.float32),
            pltpu.VMEM((n, 1, LANES), jnp.float32),
            pltpu.VMEM((n * (zh - 1), 1, LANES), jnp.float32),
            dma((3,)),
            dma((2, 2)), dma((2, 2)),
            dma((2, 2)), dma((2, 2)),
            dma((4, 2)), dma((4, 2)),
            dma((n, ny - 1)), dma((n, ny - 1)),
            dma((n, zl - 1)), dma((n, zl - 1)),
            dma((n, zh - 1)), dma((n, zh - 1)),
            dma((n, ny - 1)), dma((n, ny - 1)),
            dma((n, zl - 1)), dma((n, zl - 1)),
            dma((n, zh - 1)), dma((n, zh - 1)),
            pltpu.SemaphoreType.REGULAR, pltpu.SemaphoreType.REGULAR,
        ],
        compiler_params=pltpu.CompilerParams(
            collective_id=0, has_side_effects=True, vmem_limit_bytes=53 * 1024 * 1024),
        cost_estimate=pl.CostEstimate(
            flops=2 * tokens * feats * nx * 4 * width, bytes_accessed=2 * tokens * feats, transcendentals=0),
    )(activations, targets.T)


def solution(mesh, sizes=(NX, NY, ZH, ZL)):
    return jax.shard_map(
        functools.partial(shards, sizes),
        mesh=mesh,
        in_specs=(P("tok", "feat"), P("tok", "feat")),
        out_specs=(P(("feat", "tok"), None), P(("feat", "tok"), None)),
        check_vma=False,
    )
```

```python
import functools

import jax
import jax.numpy as jnp
from jax import lax
from jax.experimental import pallas as pl
from jax.experimental.pallas import tpu as pltpu
from jax.sharding import PartitionSpec as P

MESH = pl.DeviceIdType.MESH
NX, NY, ZH, ZL = 4, 4, 4, 4
OWN, LEFT, RIGHT, OPP = range(4)
STAGES = (((OWN, 0), (OWN, 1)), ((LEFT, 0), (RIGHT, 0)), ((LEFT, 1), (RIGHT, 1)), ((OPP, 0), (OPP, 1)))
PIECES = ((0, 0, ZH), (1, 0, ZH), (2, 0, ZH // 2), (2, ZH // 2, ZH // 2), (3, 0, 1), (3, 1, 1), (3, 2, ZH - 2))
LANES = 128
POWER, TOP = 12, 10.5


def packed(values):
    most = jnp.max(jnp.abs(values), axis=(0, 1), keepdims=True)
    scale = jnp.floor(TOP - jnp.log2(jnp.maximum(most, 1e-30)))
    x = values * jnp.exp2(scale)
    x2 = x * x
    x4 = x2 * x2
    code = x4 * x4 * x4
    code = jnp.where(x < 0, -code, code).astype(jnp.bfloat16)
    return code, jnp.broadcast_to(scale, (1, LANES))


def unpacked(code, scale):
    code = code.astype(jnp.float32)
    scale = jnp.concatenate([scale] * (code.shape[1] // LANES), axis=1)
    size = jnp.exp2(jnp.log2(jnp.maximum(jnp.abs(code), 1e-37)) * (1.0 / POWER) - scale)
    return jnp.where(code > 0, size, jnp.where(code < 0, -size, 0.0))


def kernel(
    sizes, a_hbm, t_hbm, gram_ref, cross_ref,
    a_ref, t_ref, at_ref, g_ref, ysend, yrecv, yown, asend, arecv, aown, bsend, brecv, bown, fin,
    yexp, yexps, aexp, aexps, bexp, bexps,
    in_sem, gs_sem, gr_sem, fs_sem, fr_sem, cs_sem, cr_sem, ys_sem, yr_sem, as_sem, ar_sem, bs_sem, br_sem,
    ye_sem, yf_sem, ae_sem, af_sem, be_sem, bf_sem, near_sem, far_sem,
):
    nx, ny, zh, zl = sizes
    tok, feat = lax.axis_index("tok"), lax.axis_index("feat")
    x, core = feat // 2, lax.rem(feat, 2)
    y, z = tok // (zh * zl), lax.rem(tok, zh * zl)
    shift = zl // 2 * core
    turned = lax.rem(z + shift, zh * zl)
    h, l = turned // zl, lax.rem(turned, zl)
    tokens, feats = a_ref.shape
    half, quarter = tokens // 2, tokens // 4
    width = t_ref.shape[0]
    yrows, arows, brows = feats // ny, feats // (ny * zl), feats // (ny * zl * zh)

    def at(dx=0, dy=0, dl=0, dh=0, on=core):
        xx = lax.rem(x + dx + nx, nx)
        yy = lax.rem(y + dy, ny)
        zz = lax.rem(h + dh, zh) * zl + lax.rem(l + dl, zl)
        zz = lax.rem(zz + zh * zl - shift, zh * zl)
        return {"tok": yy * (zh * zl) + zz, "feat": xx * 2 + on}

    partner = at(on=1 - core)
    first = pltpu.make_async_copy(a_hbm.at[:, pl.ds(0, 2 * width)], a_ref.at[:, pl.ds(0, 2 * width)], in_sem.at[0])
    mine = pltpu.make_async_copy(t_hbm, t_ref, in_sem.at[1])
    rest = pltpu.make_async_copy(
        a_hbm.at[:, pl.ds(2 * width, feats - 2 * width)],
        a_ref.at[:, pl.ds(2 * width, feats - 2 * width)], in_sem.at[2])
    first.start()
    mine.start()

    barrier = pltpu.get_barrier_semaphore()
    near = [dict(dx=1), dict(dx=-1)] + [dict(dy=k) for k in range(1, ny)]
    far = [dict(dl=k) for k in range(1, zl)] + [dict(dh=k) for k in range(1, zh)]
    for there in near:
        pl.semaphore_signal(barrier, inc=1, device_id=at(on=1, **there), device_id_type=MESH)
    for there in far:
        pl.semaphore_signal(barrier, inc=1, device_id=at(on=0, **there), device_id_type=MESH)

    @pl.when(core == 0)
    def _():
        pl.semaphore_signal(barrier, inc=1, device_id=partner, device_id_type=MESH)

    first.wait()
    mine.wait()
    rest.start()
    own = g_ref.at[OWN, core]
    own[...] = jnp.concatenate([a_ref[:, pl.ds(0, width)], t_ref[...].T], axis=1)

    @pl.when(core == 1)
    def _():
        pl.semaphore_wait(barrier, 2 * len(near) + 1)
        pl.semaphore_signal(near_sem, inc=1, device_id=partner, device_id_type=MESH)

    @pl.when(core == 0)
    def _():
        pl.semaphore_wait(near_sem, 1)

    def meet_far():
        @pl.when(core == 0)
        def _():
            pl.semaphore_wait(barrier, 2 * len(far))
            pl.semaphore_signal(far_sem, inc=1, device_id=partner, device_id_type=MESH)

        @pl.when(core == 1)
        def _():
            pl.semaphore_wait(far_sem, 1)

    def remote(src, dst, send, recv, peer):
        return pltpu.make_async_remote_copy(
            src_ref=src, dst_ref=dst, send_sem=send, recv_sem=recv, device_id=peer, device_id_type=MESH)

    def rows(part):
        return pl.ds(pl.multiple_of(part * half, half), half)

    def rows4(part, q):
        return pl.ds(pl.multiple_of(part * half + q * quarter, quarter), quarter)

    def hop(slot, b):
        return remote(g_ref.at[OWN, b, rows(core)], g_ref.at[slot, b, rows(core)],
                      gs_sem.at[slot - 1, b], gr_sem.at[slot - 1, b], at(dx=1 if slot == LEFT else -1))

    def forward(slot, b):
        part = rows4(core, slot - 1)
        return remote(g_ref.at[slot, b, part], g_ref.at[OPP, b, part],
                      fs_sem.at[slot - 1, b], fr_sem.at[slot - 1, b], at(dx=1 if slot == LEFT else -1))

    def share(part):
        block = g_ref.at[OWN, core, rows(part)]
        return remote(block, block, cs_sem.at[OWN, part], cr_sem.at[OWN, part], partner)

    def shared(part):
        block = g_ref.at[OWN, 1 - core, rows(part)]
        return remote(block, block, cs_sem.at[OWN, part], cr_sem.at[OWN, part], partner)

    def across(slot, b):
        block = g_ref.at[slot, b, rows(core)]
        return remote(block, block, cs_sem.at[slot, b], cr_sem.at[slot, b], partner)

    def crossed(slot, b):
        block = g_ref.at[slot, b, rows(1 - core)]
        return remote(block, block, cs_sem.at[slot, b], cr_sem.at[slot, b], partner)

    share(1 - core).start()
    share(core).start()

    @pl.when(core == 0)
    def _():
        hop(LEFT, 0).start()
        hop(RIGHT, 0).start()

    shared(core).wait_recv()

    @pl.when(core == 1)
    def _():
        hop(LEFT, 0).start()
        hop(RIGHT, 0).start()

    hop(LEFT, 1).start()
    hop(RIGHT, 1).start()

    rest.wait()
    tile = 128

    def transpose(i, carry):
        columns = pl.ds(pl.multiple_of(i * tile, tile), tile)
        at_ref[columns, :] = a_ref[:, columns].T
        return carry

    lax.fori_loop(0, feats // tile, transpose, 0)

    def ycopies(p, k):
        part = pl.ds(0, PIECES[p][2] * zl * brows)
        return (remote(ysend.at[p, k - 1, part], yrecv.at[p, k - 1, part],
                       ys_sem.at[p, k - 1], yr_sem.at[p, k - 1], at(dy=k)),
                remote(yexp.at[p * (ny - 1) + k - 1], yexps.at[p * (ny - 1) + k - 1],
                       ye_sem.at[p, k - 1], yf_sem.at[p, k - 1], at(dy=k)))

    def acopies(p, k):
        size = PIECES[p][2] * brows
        there = pl.ds(pl.multiple_of(lax.rem(l + k, zl) * size, brows), size)
        return (remote(asend.at[p, there], arecv.at[p, k - 1, pl.ds(0, size)],
                       as_sem.at[p, k - 1], ar_sem.at[p, k - 1], at(dl=k)),
                remote(aexp.at[p], aexps.at[p * (zl - 1) + k - 1],
                       ae_sem.at[p, k - 1], af_sem.at[p, k - 1], at(dl=k)))

    def bcopies(p, k):
        _, low, count = PIECES[p]
        place = lax.rem(lax.rem(h + k, zh) - low + zh, zh) if count > 1 else 0
        there = pl.ds(pl.multiple_of(lax.rem(place, count) * brows, brows), brows)
        return (remote(bsend.at[p, there], brecv.at[p, k - 1],
                       bs_sem.at[p, k - 1], br_sem.at[p, k - 1], at(dh=k)),
                remote(bexp.at[p], bexps.at[p * (zh - 1) + k - 1],
                       be_sem.at[p, k - 1], bf_sem.at[p, k - 1], at(dh=k)))

    def start(copies):
        for copy in copies:
            copy.start()

    def arrive(copies):
        for copy in copies:
            copy.wait_recv()

    def leave(copies):
        for copy in copies:
            copy.wait_send()

    def multiply(p):
        stage, low, count = PIECES[p]
        size = count * zl * brows
        both = jnp.concatenate([g_ref[slot, b] for slot, b in STAGES[stage]], axis=1)
        order = [2, 1, 3, 0] if ny == 4 else [*range(1, ny), 0]
        at_once = yrows // size
        for first_k in range(0, ny, at_once):
            group = order[first_k : first_k + at_once]
            parts = []
            for k in group:
                base = lax.rem(y + k, ny) * yrows
                for ll in range(zl):
                    for g in range(low, low + count):
                        owner = lax.rem(g * zl + ll + zh * zl - shift, zh * zl)
                        parts.append(at_ref[pl.ds(pl.multiple_of(base + owner * brows, brows), brows), :])
            terms = jnp.dot(jnp.concatenate(parts, axis=0), both, preferred_element_type=jnp.float32)
            for i, k in enumerate(group):
                term = terms[i * size : (i + 1) * size]
                if k == 0:
                    yown[p, pl.ds(0, size), :] = term
                    continue
                code, exponent = packed(term)
                ysend[p, k - 1, pl.ds(0, size), :] = code
                yexp[p * (ny - 1) + k - 1] = exponent
                start(ycopies(p, k))

    def sum_y(p):
        size, asize = PIECES[p][2] * zl * brows, PIECES[p][2] * brows
        total = yown[p, pl.ds(0, size), :]
        for k in range(1, ny):
            arrive(ycopies(p, k))
            total += unpacked(yrecv[p, k - 1, pl.ds(0, size), :], yexps[p * (ny - 1) + k - 1])
        code, exponent = packed(total)
        asend[p, pl.ds(0, size), :] = code
        aexp[p] = exponent
        if p == 0:
            meet_far()
        for k in range(1, zl):
            start(acopies(p, k))
        yown[p, pl.ds(0, size), :] = total
        aown[p, pl.ds(0, asize), :] = yown[p, pl.ds(pl.multiple_of(l * asize, brows), asize), :]

    def inside(p, g):
        _, low, count = PIECES[p]
        return (g >= low) & (g < low + count)

    def sum_a(p):
        asize = PIECES[p][2] * brows
        total = aown[p, pl.ds(0, asize), :]
        for k in range(1, zl):
            arrive(acopies(p, k))
            total += unpacked(arecv[p, k - 1, pl.ds(0, asize), :], aexps[p * (zl - 1) + k - 1])
        code, exponent = packed(total)
        bsend[p, pl.ds(0, asize), :] = code
        bexp[p] = exponent
        for k in range(1, zh):
            @pl.when(inside(p, lax.rem(h + k, zh)))
            def _():
                start(bcopies(p, k))
        bown[p, pl.ds(0, asize), :] = total

    def sum_b(p):
        stage, low, count = PIECES[p]

        @pl.when(inside(p, h))
        def _():
            mine = lax.rem(h - low + zh, zh) if count > 1 else 0
            total = bown[p, pl.ds(pl.multiple_of(lax.rem(mine, count) * brows, brows), brows), :]
            for k in range(1, zh):
                arrive(bcopies(p, k))
                total += unpacked(brecv[p, k - 1], bexps[p * (zh - 1) + k - 1])
            fin[stage] = total

    def sent_b(p):
        for k in range(1, zh):
            @pl.when(inside(p, lax.rem(h + k, zh)))
            def _():
                leave(bcopies(p, k))

    def finish(dx, places):
        chip = lax.rem(x + dx, nx)
        columns = pl.ds(pl.multiple_of(chip * 2 * width, 2 * width), 2 * width)
        for out, skip in ((gram_ref, 0), (cross_ref, width)):
            out[:, columns] = jnp.concatenate(
                [fin[stage][:, side * 2 * width + skip : side * 2 * width + skip + width] for stage, side in places],
                axis=1)

    def take(b):
        for slot in (LEFT, RIGHT):
            hop(slot, b).wait_recv()
            across(slot, b).start()
            forward(slot, b).start()

    shared(1 - core).wait_recv()
    multiply(0)
    take(0)
    for slot in (LEFT, RIGHT):
        crossed(slot, 0).wait_recv()
    multiply(1)
    sum_y(0)
    take(1)
    for slot in (LEFT, RIGHT):
        crossed(slot, 1).wait_recv()
    multiply(2)
    multiply(3)
    sum_a(0)
    for b in range(2):
        for slot in (LEFT, RIGHT):
            forward(slot, b).wait_recv()
        across(OPP, b).start()
    sum_y(1)
    for b in range(2):
        crossed(OPP, b).wait_recv()
    multiply(4)
    sum_y(2)
    multiply(5)
    multiply(6)
    sum_y(3)
    sum_a(1)
    sum_y(4)
    sum_a(2)
    sum_y(5)
    sum_a(3)
    sum_a(4)
    sum_a(5)
    sum_y(6)
    sum_b(0)
    finish(0, ((0, 0), (0, 1)))
    sum_a(6)
    sum_b(1)
    sum_b(2)
    sum_b(3)
    finish(nx - 1, ((1, 0), (2, 0)))
    finish(1, ((1, 1), (2, 1)))
    sum_b(4)
    sum_b(5)
    sum_b(6)
    finish(nx // 2, ((3, 0), (3, 1)))

    for part in range(2):
        share(part).wait_send()
    for b in range(2):
        for slot in (LEFT, RIGHT):
            hop(slot, b).wait_send()
            forward(slot, b).wait_send()
        for slot in (LEFT, RIGHT, OPP):
            across(slot, b).wait_send()
    for p in range(len(PIECES)):
        for k in range(1, ny):
            leave(ycopies(p, k))
        for k in range(1, zl):
            leave(acopies(p, k))
        sent_b(p)


def shards(sizes, activations, targets):
    nx, ny, zh, zl = sizes
    tokens, feats = activations.shape
    width = targets.shape[1]
    two, n = 4 * width, len(PIECES)
    yrows, arows, brows = feats // ny, feats // (ny * zl), feats // (ny * zl * zh)
    out = jax.ShapeDtypeStruct((brows, nx * 2 * width), jnp.float32)
    dma = pltpu.SemaphoreType.DMA
    return pl.pallas_call(
        functools.partial(kernel, sizes),
        out_shape=(out, out),
        in_specs=[pl.BlockSpec(memory_space=pl.ANY)] * 2,
        out_specs=(pl.BlockSpec(memory_space=pltpu.VMEM),) * 2,
        scratch_shapes=[
            pltpu.VMEM((tokens, feats), jnp.bfloat16),
            pltpu.VMEM((width, tokens), jnp.bfloat16),
            pltpu.VMEM((feats, tokens), jnp.bfloat16),
            pltpu.VMEM((4, 2, tokens, 2 * width), jnp.bfloat16),
            pltpu.VMEM((n, ny - 1, yrows, two), jnp.bfloat16),
            pltpu.VMEM((n, ny - 1, yrows, two), jnp.bfloat16),
            pltpu.VMEM((n, yrows, two), jnp.float32),
            pltpu.VMEM((n, yrows, two), jnp.bfloat16),
            pltpu.VMEM((n, zl - 1, arows, two), jnp.bfloat16),
            pltpu.VMEM((n, arows, two), jnp.float32),
            pltpu.VMEM((n, arows, two), jnp.bfloat16),
            pltpu.VMEM((n, zh - 1, brows, two), jnp.bfloat16),
            pltpu.VMEM((n, arows, two), jnp.float32),
            pltpu.VMEM((4, brows, two), jnp.float32),
            pltpu.VMEM((n * (ny - 1), 1, LANES), jnp.float32),
            pltpu.VMEM((n * (ny - 1), 1, LANES), jnp.float32),
            pltpu.VMEM((n, 1, LANES), jnp.float32),
            pltpu.VMEM((n * (zl - 1), 1, LANES), jnp.float32),
            pltpu.VMEM((n, 1, LANES), jnp.float32),
            pltpu.VMEM((n * (zh - 1), 1, LANES), jnp.float32),
            dma((3,)),
            dma((2, 2)), dma((2, 2)),
            dma((2, 2)), dma((2, 2)),
            dma((4, 2)), dma((4, 2)),
            dma((n, ny - 1)), dma((n, ny - 1)),
            dma((n, zl - 1)), dma((n, zl - 1)),
            dma((n, zh - 1)), dma((n, zh - 1)),
            dma((n, ny - 1)), dma((n, ny - 1)),
            dma((n, zl - 1)), dma((n, zl - 1)),
            dma((n, zh - 1)), dma((n, zh - 1)),
            pltpu.SemaphoreType.REGULAR, pltpu.SemaphoreType.REGULAR,
        ],
        compiler_params=pltpu.CompilerParams(
            collective_id=0, has_side_effects=True, vmem_limit_bytes=55104 * 1024),
        cost_estimate=pl.CostEstimate(
            flops=2 * tokens * feats * nx * 4 * width, bytes_accessed=2 * tokens * feats, transcendentals=0),
    )(activations, targets.T)


def solution(mesh, sizes=(NX, NY, ZH, ZL)):
    return jax.shard_map(
        functools.partial(shards, sizes),
        mesh=mesh,
        in_specs=(P("tok", "feat"), P("tok", "feat")),
        out_specs=(P(("feat", "tok"), None), P(("feat", "tok"), None)),
        check_vma=False,
    )
```

```python
import functools

import jax
import jax.numpy as jnp
from jax import lax
from jax.experimental import pallas as pl
from jax.experimental.pallas import tpu as pltpu
from jax.sharding import PartitionSpec as P

MESH = pl.DeviceIdType.MESH
NX, NY, ZH, ZL = 4, 4, 4, 4
OWN, LEFT, RIGHT, OPP = range(4)
STAGES = (((OWN, 0), (OWN, 1)), ((LEFT, 0), (RIGHT, 0)), ((LEFT, 1), (RIGHT, 1)), ((OPP, 0), (OPP, 1)))
PIECES = ((0, 0, ZH), (1, 0, ZH), (2, 0, ZH // 2), (2, ZH // 2, ZH // 2), (3, 0, 1), (3, 1, 1), (3, 2, ZH - 2))
LANES = 128
PAD = 16
POWER, TOP = 12, 10.5


def packed(values):
    most = jnp.max(jnp.abs(values), axis=(0, 1), keepdims=True)
    scale = jnp.floor(TOP - jnp.log2(jnp.maximum(most, 1e-30)))
    x = values * jnp.exp2(scale)
    x2 = x * x
    x4 = x2 * x2
    code = x4 * x4 * x4
    code = jnp.where(x < 0, -code, code).astype(jnp.bfloat16)
    exponent = jnp.broadcast_to(scale, (PAD, LANES)).astype(jnp.bfloat16)
    return jnp.concatenate([code[:, :LANES], code[:, LANES:], exponent], axis=0)


def unpacked(sent):
    rows = (sent.shape[0] - PAD) // 2
    sent = sent.astype(jnp.float32)
    code, scale = sent[: 2 * rows], sent[2 * rows : 2 * rows + 1]
    size = jnp.exp2(jnp.log2(jnp.maximum(jnp.abs(code), 1e-37)) * (1.0 / POWER) - scale)
    values = jnp.where(code > 0, size, jnp.where(code < 0, -size, 0.0))
    return jnp.concatenate([values[:rows], values[rows:]], axis=1)


def kernel(
    sizes, a_hbm, t_hbm, out_ref,
    a_ref, t_ref, at_ref, g_ref, ysend, yrecv, yown, asend, arecv, aown, bsend, brecv, bown, fin,
    in_sem, gs_sem, gr_sem, fs_sem, fr_sem, cs_sem, cr_sem, ys_sem, yr_sem, as_sem, ar_sem, bs_sem, br_sem,
    near_sem, far_sem,
):
    nx, ny, zh, zl = sizes
    tok, feat = lax.axis_index("tok"), lax.axis_index("feat")
    x, core = feat // 2, lax.rem(feat, 2)
    y, z = tok // (zh * zl), lax.rem(tok, zh * zl)
    shift = zl // 2 * core
    turned = lax.rem(z + shift, zh * zl)
    h, l = turned // zl, lax.rem(turned, zl)
    tokens, feats = a_ref.shape
    half, quarter = tokens // 2, tokens // 4
    width = t_ref.shape[0]
    yrows, arows, brows = feats // ny, feats // (ny * zl), feats // (ny * zl * zh)

    def at(dx=0, dy=0, dl=0, dh=0, on=core):
        xx = lax.rem(x + dx + nx, nx)
        yy = lax.rem(y + dy, ny)
        zz = lax.rem(h + dh, zh) * zl + lax.rem(l + dl, zl)
        zz = lax.rem(zz + zh * zl - shift, zh * zl)
        return {"tok": yy * (zh * zl) + zz, "feat": xx * 2 + on}

    partner = at(on=1 - core)
    first = pltpu.make_async_copy(a_hbm.at[:, pl.ds(0, 2 * width)], a_ref.at[:, pl.ds(0, 2 * width)], in_sem.at[0])
    mine = pltpu.make_async_copy(t_hbm, t_ref, in_sem.at[1])
    rest = pltpu.make_async_copy(
        a_hbm.at[:, pl.ds(2 * width, feats - 2 * width)],
        a_ref.at[:, pl.ds(2 * width, feats - 2 * width)], in_sem.at[2])
    first.start()
    mine.start()

    barrier = pltpu.get_barrier_semaphore()
    near = [dict(dx=1), dict(dx=-1)] + [dict(dy=k) for k in range(1, ny)]
    far = [dict(dl=k) for k in range(1, zl)] + [dict(dh=k) for k in range(1, zh)]
    for there in near:
        pl.semaphore_signal(barrier, inc=1, device_id=at(on=1, **there), device_id_type=MESH)

    @pl.when(core == 0)
    def _():
        pl.semaphore_signal(barrier, inc=1, device_id=partner, device_id_type=MESH)

    first.wait()
    mine.wait()
    rest.start()
    own = g_ref.at[OWN, core]
    own[...] = jnp.concatenate([a_ref[:, pl.ds(0, width)], t_ref[...].T], axis=1)

    @pl.when(core == 1)
    def _():
        pl.semaphore_wait(barrier, 2 * len(near) + 1)
        pl.semaphore_signal(near_sem, inc=1, device_id=partner, device_id_type=MESH)

    @pl.when(core == 0)
    def _():
        pl.semaphore_wait(near_sem, 1)

    def meet_far():
        @pl.when(core == 0)
        def _():
            pl.semaphore_wait(barrier, 2 * len(far))
            pl.semaphore_signal(far_sem, inc=1, device_id=partner, device_id_type=MESH)

        @pl.when(core == 1)
        def _():
            pl.semaphore_wait(far_sem, 1)

    def remote(src, dst, send, recv, peer):
        return pltpu.make_async_remote_copy(
            src_ref=src, dst_ref=dst, send_sem=send, recv_sem=recv, device_id=peer, device_id_type=MESH)

    def rows(part):
        return pl.ds(pl.multiple_of(part * half, half), half)

    def rows4(part, q):
        return pl.ds(pl.multiple_of(part * half + q * quarter, quarter), quarter)

    def hop(slot, b):
        return remote(g_ref.at[OWN, b, rows(core)], g_ref.at[slot, b, rows(core)],
                      gs_sem.at[slot - 1, b], gr_sem.at[slot - 1, b], at(dx=1 if slot == LEFT else -1))

    def forward(slot, b):
        part = rows4(core, slot - 1)
        return remote(g_ref.at[slot, b, part], g_ref.at[OPP, b, part],
                      fs_sem.at[slot - 1, b], fr_sem.at[slot - 1, b], at(dx=1 if slot == LEFT else -1))

    def share(part):
        block = g_ref.at[OWN, core, rows(part)]
        return remote(block, block, cs_sem.at[OWN, part], cr_sem.at[OWN, part], partner)

    def shared(part):
        block = g_ref.at[OWN, 1 - core, rows(part)]
        return remote(block, block, cs_sem.at[OWN, part], cr_sem.at[OWN, part], partner)

    def across(slot, b):
        block = g_ref.at[slot, b, rows(core)]
        return remote(block, block, cs_sem.at[slot, b], cr_sem.at[slot, b], partner)

    def crossed(slot, b):
        block = g_ref.at[slot, b, rows(1 - core)]
        return remote(block, block, cs_sem.at[slot, b], cr_sem.at[slot, b], partner)

    share(1 - core).start()

    @pl.when(core == 0)
    def _():
        hop(LEFT, 0).start()
        hop(RIGHT, 0).start()

    share(core).start()

    shared(core).wait_recv()

    @pl.when(core == 1)
    def _():
        hop(LEFT, 0).start()
        hop(RIGHT, 0).start()

    hop(LEFT, 1).start()
    hop(RIGHT, 1).start()
    for there in far:
        pl.semaphore_signal(barrier, inc=1, device_id=at(on=0, **there), device_id_type=MESH)

    rest.wait()
    tile = 128

    def transpose(i, carry):
        columns = pl.ds(pl.multiple_of(i * tile, tile), tile)
        at_ref[columns, :] = a_ref[:, columns].T
        return carry

    lax.fori_loop(0, feats // tile, transpose, 0)

    def ycopy(p, k):
        part = pl.ds(0, 2 * PIECES[p][2] * zl * brows + PAD)
        return remote(ysend.at[p, k - 1, part], yrecv.at[p, k - 1, part],
                      ys_sem.at[p, k - 1], yr_sem.at[p, k - 1], at(dy=k))

    def acopy(p, k):
        part = pl.ds(0, 2 * PIECES[p][2] * brows + PAD)
        return remote(asend.at[p, lax.rem(l + k, zl), part], arecv.at[p, k - 1, part],
                      as_sem.at[p, k - 1], ar_sem.at[p, k - 1], at(dl=k))

    def bcopy(p, k):
        _, low, count = PIECES[p]
        place = lax.rem(lax.rem(lax.rem(h + k, zh) - low + zh, zh), count)
        return remote(bsend.at[p, place], brecv.at[p, k - 1], bs_sem.at[p, k - 1], br_sem.at[p, k - 1], at(dh=k))

    def multiply(p):
        stage, low, count = PIECES[p]
        size = count * zl * brows
        both = jnp.concatenate([g_ref[slot, b] for slot, b in STAGES[stage]], axis=1)
        order = [2, 1, 3, 0] if ny == 4 else [*range(1, ny), 0]
        at_once = yrows // size
        for first_k in range(0, ny, at_once):
            group = order[first_k : first_k + at_once]
            parts = []
            for k in group:
                base = lax.rem(y + k, ny) * yrows
                for ll in range(zl):
                    for g in range(low, low + count):
                        owner = lax.rem(g * zl + ll + zh * zl - shift, zh * zl)
                        parts.append(at_ref[pl.ds(pl.multiple_of(base + owner * brows, brows), brows), :])
            terms = jnp.dot(jnp.concatenate(parts, axis=0), both, preferred_element_type=jnp.float32)
            for i, k in enumerate(group):
                term = terms[i * size : (i + 1) * size]
                if k == 0:
                    yown[p, pl.ds(0, size), :] = term
                    continue
                ysend[p, k - 1, pl.ds(0, 2 * size + PAD), :] = packed(term)
                ycopy(p, k).start()

    def sum_y(p):
        size, asize = PIECES[p][2] * zl * brows, PIECES[p][2] * brows
        total = yown[p, pl.ds(0, size), :]
        for k in range(1, ny):
            ycopy(p, k).wait_recv()
            total += unpacked(yrecv[p, k - 1, pl.ds(0, 2 * size + PAD), :])
        for ll in range(zl):
            asend[p, ll, pl.ds(0, 2 * asize + PAD), :] = packed(total[ll * asize : (ll + 1) * asize])
        if p == 0:
            meet_far()
        for k in range(1, zl):
            acopy(p, k).start()
        yown[p, pl.ds(0, size), :] = total
        aown[p, pl.ds(0, asize), :] = yown[p, pl.ds(pl.multiple_of(l * asize, brows), asize), :]

    def inside(p, g):
        _, low, count = PIECES[p]
        return (g >= low) & (g < low + count)

    def sum_a(p):
        asize = PIECES[p][2] * brows
        total = aown[p, pl.ds(0, asize), :]
        for k in range(1, zl):
            acopy(p, k).wait_recv()
            total += unpacked(arecv[p, k - 1, pl.ds(0, 2 * asize + PAD), :])
        for g in range(PIECES[p][2]):
            bsend[p, g] = packed(total[g * brows : (g + 1) * brows])
        for k in range(1, zh):
            @pl.when(inside(p, lax.rem(h + k, zh)))
            def _():
                bcopy(p, k).start()
        bown[p, pl.ds(0, asize), :] = total

    def sum_b(p):
        stage, low, count = PIECES[p]

        @pl.when(inside(p, h))
        def _():
            mine = lax.rem(h - low + zh, zh) if count > 1 else 0
            total = bown[p, pl.ds(pl.multiple_of(lax.rem(mine, count) * brows, brows), brows), :]
            for k in range(1, zh):
                bcopy(p, k).wait_recv()
                total += unpacked(brecv[p, k - 1])
            fin[stage] = total

    def sent_b(p):
        for k in range(1, zh):
            @pl.when(inside(p, lax.rem(h + k, zh)))
            def _():
                bcopy(p, k).wait_send()

    def finish(dx, places):
        chip = lax.rem(x + dx, nx)
        columns = pl.ds(pl.multiple_of(chip * 2 * width, 2 * width), 2 * width)
        for top, skip in ((0, 0), (brows, width)):
            out_ref[pl.ds(top, brows), columns] = jnp.concatenate(
                [fin[stage][:, side * 2 * width + skip : side * 2 * width + skip + width] for stage, side in places],
                axis=1)

    def take(b):
        for slot in (LEFT, RIGHT):
            hop(slot, b).wait_recv()
            across(slot, b).start()
            forward(slot, b).start()

    shared(1 - core).wait_recv()
    multiply(0)
    take(0)
    for slot in (LEFT, RIGHT):
        crossed(slot, 0).wait_recv()
    multiply(1)
    sum_y(0)
    take(1)
    for slot in (LEFT, RIGHT):
        crossed(slot, 1).wait_recv()
    multiply(2)
    multiply(3)
    sum_a(0)
    for b in range(2):
        for slot in (LEFT, RIGHT):
            forward(slot, b).wait_recv()
        across(OPP, b).start()
    sum_y(1)
    for b in range(2):
        crossed(OPP, b).wait_recv()
    multiply(4)
    sum_y(2)
    multiply(5)
    multiply(6)
    sum_y(3)
    sum_a(1)
    sum_y(4)
    sum_a(2)
    sum_y(5)
    sum_a(3)
    sum_a(4)
    sum_a(5)
    sum_y(6)
    sum_b(0)
    finish(0, ((0, 0), (0, 1)))
    sum_a(6)
    sum_b(1)
    sum_b(2)
    sum_b(3)
    finish(nx - 1, ((1, 0), (2, 0)))
    finish(1, ((1, 1), (2, 1)))
    sum_b(4)
    sum_b(5)
    sum_b(6)
    finish(nx // 2, ((3, 0), (3, 1)))

    for part in range(2):
        share(part).wait_send()
    for b in range(2):
        for slot in (LEFT, RIGHT):
            hop(slot, b).wait_send()
            forward(slot, b).wait_send()
        for slot in (LEFT, RIGHT, OPP):
            across(slot, b).wait_send()
    for p in range(len(PIECES)):
        for k in range(1, ny):
            ycopy(p, k).wait_send()
        for k in range(1, zl):
            acopy(p, k).wait_send()
        sent_b(p)


def shards(sizes, activations, targets):
    nx, ny, zh, zl = sizes
    tokens, feats = activations.shape
    width = targets.shape[1]
    two, n = 4 * width, len(PIECES)
    yrows, arows, brows = feats // ny, feats // (ny * zl), feats // (ny * zl * zh)
    out = jax.ShapeDtypeStruct((2 * brows, nx * 2 * width), jnp.float32)
    dma = pltpu.SemaphoreType.DMA
    both = pl.pallas_call(
        functools.partial(kernel, sizes),
        out_shape=out,
        in_specs=[pl.BlockSpec(memory_space=pl.ANY)] * 2,
        out_specs=pl.BlockSpec(memory_space=pltpu.VMEM),
        scratch_shapes=[
            pltpu.VMEM((tokens, feats), jnp.bfloat16),
            pltpu.VMEM((width, tokens), jnp.bfloat16),
            pltpu.VMEM((feats, tokens), jnp.bfloat16),
            pltpu.VMEM((4, 2, tokens, 2 * width), jnp.bfloat16),
            pltpu.VMEM((n, ny - 1, 2 * yrows + PAD, LANES), jnp.bfloat16),
            pltpu.VMEM((n, ny - 1, 2 * yrows + PAD, LANES), jnp.bfloat16),
            pltpu.VMEM((n, yrows, two), jnp.float32),
            pltpu.VMEM((n, zl, 2 * arows + PAD, LANES), jnp.bfloat16),
            pltpu.VMEM((n, zl - 1, 2 * arows + PAD, LANES), jnp.bfloat16),
            pltpu.VMEM((n, arows, two), jnp.float32),
            pltpu.VMEM((n, zh, 2 * brows + PAD, LANES), jnp.bfloat16),
            pltpu.VMEM((n, zh - 1, 2 * brows + PAD, LANES), jnp.bfloat16),
            pltpu.VMEM((n, arows, two), jnp.float32),
            pltpu.VMEM((4, brows, two), jnp.float32),
            dma((3,)),
            dma((2, 2)), dma((2, 2)),
            dma((2, 2)), dma((2, 2)),
            dma((4, 2)), dma((4, 2)),
            dma((n, ny - 1)), dma((n, ny - 1)),
            dma((n, zl - 1)), dma((n, zl - 1)),
            dma((n, zh - 1)), dma((n, zh - 1)),
            pltpu.SemaphoreType.REGULAR, pltpu.SemaphoreType.REGULAR,
        ],
        compiler_params=pltpu.CompilerParams(
            collective_id=0, has_side_effects=True, vmem_limit_bytes=55104 * 1024),
        cost_estimate=pl.CostEstimate(
            flops=2 * tokens * feats * nx * 4 * width, bytes_accessed=2 * tokens * feats, transcendentals=0),
    )(activations, targets.T)
    return both[:brows], both[brows:]


def solution(mesh, sizes=(NX, NY, ZH, ZL)):
    return jax.shard_map(
        functools.partial(shards, sizes),
        mesh=mesh,
        in_specs=(P("tok", "feat"), P("tok", "feat")),
        out_specs=(P(("feat", "tok"), None), P(("feat", "tok"), None)),
        check_vma=False,
    )
```

```python
import functools

import jax
import jax.numpy as jnp
from jax import lax
from jax.experimental import pallas as pl
from jax.experimental.pallas import tpu as pltpu
from jax.sharding import PartitionSpec as P

MESH = pl.DeviceIdType.MESH
NX, NY, ZH, ZL = 4, 4, 4, 4
OWN, LEFT, RIGHT, OPP = range(4)
STAGES = (((OWN, 0), (OWN, 1)), ((LEFT, 0), (RIGHT, 0)), ((LEFT, 1), (RIGHT, 1)), ((OPP, 0), (OPP, 1)))
PIECES = ((0, 0, ZH), (1, 0, ZH), (2, 0, ZH // 2), (2, ZH // 2, ZH // 2), (3, 0, 1), (3, 1, 1), (3, 2, ZH - 2))
LANES = 128
PAD = 16
POWER, TOP = 12, 10.5


def packed(values):
    most = jnp.max(jnp.abs(values), axis=(0, 1), keepdims=True)
    scale = jnp.floor(TOP - jnp.log2(jnp.maximum(most, 1e-30)))
    x = values * jnp.exp2(scale)
    x2 = x * x
    x4 = x2 * x2
    code = x4 * x4 * x4
    code = jnp.where(x < 0, -code, code).astype(jnp.bfloat16)
    exponent = jnp.broadcast_to(scale, (PAD, LANES)).astype(jnp.bfloat16)
    return jnp.concatenate([code[:, :LANES], code[:, LANES:], exponent], axis=0)


def unpacked(sent):
    rows = (sent.shape[0] - PAD) // 2
    sent = sent.astype(jnp.float32)
    code, scale = sent[: 2 * rows], sent[2 * rows : 2 * rows + 1]
    size = jnp.exp2(jnp.log2(jnp.maximum(jnp.abs(code), 1e-37)) * (1.0 / POWER) - scale)
    values = jnp.where(code > 0, size, jnp.where(code < 0, -size, 0.0))
    return jnp.concatenate([values[:rows], values[rows:]], axis=1)


def kernel(
    sizes, a_hbm, t_hbm, out_ref,
    a_ref, t_ref, at_ref, g_ref, ysend, yrecv, yown, asend, arecv, aown, bsend, brecv, bown, fin,
    in_sem, gs_sem, gr_sem, fs_sem, fr_sem, cs_sem, cr_sem, ys_sem, yr_sem, as_sem, ar_sem, bs_sem, br_sem,
    near_sem, far_sem,
):
    nx, ny, zh, zl = sizes
    tok, feat = lax.axis_index("tok"), lax.axis_index("feat")
    x, core = feat // 2, lax.rem(feat, 2)
    y, z = tok // (zh * zl), lax.rem(tok, zh * zl)
    shift = zl // 2 * core
    turned = lax.rem(z + shift, zh * zl)
    h, l = turned // zl, lax.rem(turned, zl)
    tokens, feats = a_ref.shape
    half, quarter = tokens // 2, tokens // 4
    width = t_ref.shape[0]
    yrows, arows, brows = feats // ny, feats // (ny * zl), feats // (ny * zl * zh)

    def at(dx=0, dy=0, dl=0, dh=0, on=core):
        xx = lax.rem(x + dx + nx, nx)
        yy = lax.rem(y + dy, ny)
        zz = lax.rem(h + dh, zh) * zl + lax.rem(l + dl, zl)
        zz = lax.rem(zz + zh * zl - shift, zh * zl)
        return {"tok": yy * (zh * zl) + zz, "feat": xx * 2 + on}

    partner = at(on=1 - core)
    first = pltpu.make_async_copy(a_hbm.at[:, pl.ds(0, 2 * width)], a_ref.at[:, pl.ds(0, 2 * width)], in_sem.at[0])
    mine = pltpu.make_async_copy(t_hbm, t_ref, in_sem.at[1])
    rest = pltpu.make_async_copy(
        a_hbm.at[:, pl.ds(2 * width, feats - 2 * width)],
        a_ref.at[:, pl.ds(2 * width, feats - 2 * width)], in_sem.at[2])
    first.start()
    mine.start()

    barrier = pltpu.get_barrier_semaphore()
    near = [dict(dx=1), dict(dx=-1)] + [dict(dy=k) for k in range(1, ny)]
    far = [dict(dl=k) for k in range(1, zl)] + [dict(dh=k) for k in range(1, zh)]
    for there in near:
        pl.semaphore_signal(barrier, inc=1, device_id=at(on=1, **there), device_id_type=MESH)

    @pl.when(core == 0)
    def _():
        pl.semaphore_signal(barrier, inc=1, device_id=partner, device_id_type=MESH)

    first.wait()
    mine.wait()
    rest.start()
    own = g_ref.at[OWN, core]
    own[...] = jnp.concatenate([a_ref[:, pl.ds(0, width)], t_ref[...].T], axis=1)

    @pl.when(core == 1)
    def _():
        pl.semaphore_wait(barrier, 2 * len(near) + 1)
        pl.semaphore_signal(near_sem, inc=1, device_id=partner, device_id_type=MESH)

    @pl.when(core == 0)
    def _():
        pl.semaphore_wait(near_sem, 1)

    def meet_far():
        @pl.when(core == 0)
        def _():
            pl.semaphore_wait(barrier, 2 * len(far))
            pl.semaphore_signal(far_sem, inc=1, device_id=partner, device_id_type=MESH)

        @pl.when(core == 1)
        def _():
            pl.semaphore_wait(far_sem, 1)

    def remote(src, dst, send, recv, peer):
        return pltpu.make_async_remote_copy(
            src_ref=src, dst_ref=dst, send_sem=send, recv_sem=recv, device_id=peer, device_id_type=MESH)

    def rows(part):
        return pl.ds(pl.multiple_of(part * half, half), half)

    def rows4(part, q):
        return pl.ds(pl.multiple_of(part * half + q * quarter, quarter), quarter)

    def hop(slot, b):
        return remote(g_ref.at[OWN, b, rows(core)], g_ref.at[slot, b, rows(core)],
                      gs_sem.at[slot - 1, b], gr_sem.at[slot - 1, b], at(dx=1 if slot == LEFT else -1))

    def forward(slot, b):
        part = rows4(core, slot - 1)
        return remote(g_ref.at[slot, b, part], g_ref.at[OPP, b, part],
                      fs_sem.at[slot - 1, b], fr_sem.at[slot - 1, b], at(dx=1 if slot == LEFT else -1))

    def share(part):
        block = g_ref.at[OWN, core, rows(part)]
        return remote(block, block, cs_sem.at[OWN, part], cr_sem.at[OWN, part], partner)

    def shared(part):
        block = g_ref.at[OWN, 1 - core, rows(part)]
        return remote(block, block, cs_sem.at[OWN, part], cr_sem.at[OWN, part], partner)

    def across(slot, b):
        block = g_ref.at[slot, b, rows(core)]
        return remote(block, block, cs_sem.at[slot, b], cr_sem.at[slot, b], partner)

    def crossed(slot, b):
        block = g_ref.at[slot, b, rows(1 - core)]
        return remote(block, block, cs_sem.at[slot, b], cr_sem.at[slot, b], partner)

    share(1 - core).start()

    @pl.when(core == 0)
    def _():
        hop(LEFT, 0).start()
        hop(RIGHT, 0).start()

    share(core).start()

    shared(core).wait_recv()

    @pl.when(core == 1)
    def _():
        hop(LEFT, 0).start()
        hop(RIGHT, 0).start()

    hop(LEFT, 1).start()
    hop(RIGHT, 1).start()
    for there in far:
        pl.semaphore_signal(barrier, inc=1, device_id=at(on=0, **there), device_id_type=MESH)

    rest.wait()
    tile = 128

    def transpose(i, carry):
        columns = pl.ds(pl.multiple_of(i * tile, tile), tile)
        at_ref[columns, :] = a_ref[:, columns].T
        return carry

    lax.fori_loop(0, feats // tile, transpose, 0)

    def ycopy(p, k):
        part = pl.ds(0, 2 * PIECES[p][2] * zl * brows + PAD)
        return remote(ysend.at[p, k - 1, part], yrecv.at[p, k - 1, part],
                      ys_sem.at[p, k - 1], yr_sem.at[p, k - 1], at(dy=k))

    def acopy(p, k):
        part = pl.ds(0, 2 * PIECES[p][2] * brows + PAD)
        return remote(asend.at[p, lax.rem(l + k, zl), part], arecv.at[p, k - 1, part],
                      as_sem.at[p, k - 1], ar_sem.at[p, k - 1], at(dl=k))

    def bcopy(p, k):
        _, low, count = PIECES[p]
        place = lax.rem(lax.rem(lax.rem(h + k, zh) - low + zh, zh), count)
        return remote(bsend.at[p, place], brecv.at[p, k - 1], bs_sem.at[p, k - 1], br_sem.at[p, k - 1], at(dh=k))

    def multiply(p):
        stage, low, count = PIECES[p]
        size = count * zl * brows
        both = jnp.concatenate([g_ref[slot, b] for slot, b in STAGES[stage]], axis=1)
        order = [2, 1, 3, 0] if ny == 4 else [*range(1, ny), 0]
        at_once = yrows // size
        for first_k in range(0, ny, at_once):
            group = order[first_k : first_k + at_once]
            parts = []
            for k in group:
                base = lax.rem(y + k, ny) * yrows
                for ll in range(zl):
                    for g in range(low, low + count):
                        owner = lax.rem(g * zl + ll + zh * zl - shift, zh * zl)
                        parts.append(at_ref[pl.ds(pl.multiple_of(base + owner * brows, brows), brows), :])
            terms = jnp.dot(jnp.concatenate(parts, axis=0), both, preferred_element_type=jnp.float32)
            for i, k in enumerate(group):
                term = terms[i * size : (i + 1) * size]
                if k == 0:
                    yown[p, pl.ds(0, size), :] = term
                    continue
                ysend[p, k - 1, pl.ds(0, 2 * size + PAD), :] = packed(term)
                ycopy(p, k).start()

    def sum_y(p):
        size, asize = PIECES[p][2] * zl * brows, PIECES[p][2] * brows
        total = yown[p, pl.ds(0, size), :]
        for k in range(1, ny):
            ycopy(p, k).wait_recv()
            total += unpacked(yrecv[p, k - 1, pl.ds(0, 2 * size + PAD), :])
        for ll in range(zl):
            asend[p, ll, pl.ds(0, 2 * asize + PAD), :] = packed(total[ll * asize : (ll + 1) * asize])
        if p == 0:
            meet_far()
        for k in range(1, zl):
            acopy(p, k).start()
        yown[p, pl.ds(0, size), :] = total
        aown[p, pl.ds(0, asize), :] = yown[p, pl.ds(pl.multiple_of(l * asize, brows), asize), :]

    def inside(p, g):
        _, low, count = PIECES[p]
        return (g >= low) & (g < low + count)

    def sum_a(p):
        asize = PIECES[p][2] * brows
        total = aown[p, pl.ds(0, asize), :]
        for k in range(1, zl):
            acopy(p, k).wait_recv()
            total += unpacked(arecv[p, k - 1, pl.ds(0, 2 * asize + PAD), :])
        for g in range(PIECES[p][2]):
            bsend[p, g] = packed(total[g * brows : (g + 1) * brows])
        for k in range(1, zh):
            @pl.when(inside(p, lax.rem(h + k, zh)))
            def _():
                bcopy(p, k).start()
        bown[p, pl.ds(0, asize), :] = total

    def sum_b(p):
        stage, low, count = PIECES[p]

        @pl.when(inside(p, h))
        def _():
            mine = lax.rem(h - low + zh, zh) if count > 1 else 0
            total = bown[p, pl.ds(pl.multiple_of(lax.rem(mine, count) * brows, brows), brows), :]
            for k in range(1, zh):
                bcopy(p, k).wait_recv()
                total += unpacked(brecv[p, k - 1])
            fin[stage] = total

    def sent_b(p):
        for k in range(1, zh):
            @pl.when(inside(p, lax.rem(h + k, zh)))
            def _():
                bcopy(p, k).wait_send()

    def finish(dx, places):
        chip = lax.rem(x + dx, nx)
        columns = pl.ds(pl.multiple_of(chip * 2 * width, 2 * width), 2 * width)
        for top, skip in ((0, 0), (brows, width)):
            out_ref[pl.ds(top, brows), columns] = jnp.concatenate(
                [fin[stage][:, side * 2 * width + skip : side * 2 * width + skip + width] for stage, side in places],
                axis=1)

    def take(b):
        for slot in (LEFT, RIGHT):
            hop(slot, b).wait_recv()
            forward(slot, b).start()
        for slot in (LEFT, RIGHT):
            across(slot, b).start()

    shared(1 - core).wait_recv()
    multiply(0)
    take(0)
    for slot in (LEFT, RIGHT):
        crossed(slot, 0).wait_recv()
    multiply(1)
    sum_y(0)
    take(1)
    for slot in (LEFT, RIGHT):
        crossed(slot, 1).wait_recv()
    multiply(2)
    multiply(3)
    sum_a(0)
    for b in range(2):
        for slot in (LEFT, RIGHT):
            forward(slot, b).wait_recv()
        across(OPP, b).start()
    sum_y(1)
    for b in range(2):
        crossed(OPP, b).wait_recv()
    multiply(4)
    sum_y(2)
    multiply(5)
    multiply(6)
    sum_y(3)
    sum_a(1)
    sum_y(4)
    sum_a(2)
    sum_y(5)
    sum_a(3)
    sum_a(4)
    sum_a(5)
    sum_y(6)
    sum_b(0)
    finish(0, ((0, 0), (0, 1)))
    sum_a(6)
    sum_b(1)
    sum_b(2)
    sum_b(3)
    finish(nx - 1, ((1, 0), (2, 0)))
    finish(1, ((1, 1), (2, 1)))
    sum_b(4)
    sum_b(5)
    sum_b(6)
    finish(nx // 2, ((3, 0), (3, 1)))

    for part in range(2):
        share(part).wait_send()
    for b in range(2):
        for slot in (LEFT, RIGHT):
            hop(slot, b).wait_send()
            forward(slot, b).wait_send()
        for slot in (LEFT, RIGHT, OPP):
            across(slot, b).wait_send()
    for p in range(len(PIECES)):
        for k in range(1, ny):
            ycopy(p, k).wait_send()
        for k in range(1, zl):
            acopy(p, k).wait_send()
        sent_b(p)


def shards(sizes, activations, targets):
    nx, ny, zh, zl = sizes
    tokens, feats = activations.shape
    width = targets.shape[1]
    two, n = 4 * width, len(PIECES)
    yrows, arows, brows = feats // ny, feats // (ny * zl), feats // (ny * zl * zh)
    out = jax.ShapeDtypeStruct((2 * brows, nx * 2 * width), jnp.float32)
    dma = pltpu.SemaphoreType.DMA
    both = pl.pallas_call(
        functools.partial(kernel, sizes),
        out_shape=out,
        in_specs=[pl.BlockSpec(memory_space=pl.ANY)] * 2,
        out_specs=pl.BlockSpec(memory_space=pltpu.VMEM),
        scratch_shapes=[
            pltpu.VMEM((tokens, feats), jnp.bfloat16),
            pltpu.VMEM((width, tokens), jnp.bfloat16),
            pltpu.VMEM((feats, tokens), jnp.bfloat16),
            pltpu.VMEM((4, 2, tokens, 2 * width), jnp.bfloat16),
            pltpu.VMEM((n, ny - 1, 2 * yrows + PAD, LANES), jnp.bfloat16),
            pltpu.VMEM((n, ny - 1, 2 * yrows + PAD, LANES), jnp.bfloat16),
            pltpu.VMEM((n, yrows, two), jnp.float32),
            pltpu.VMEM((n, zl, 2 * arows + PAD, LANES), jnp.bfloat16),
            pltpu.VMEM((n, zl - 1, 2 * arows + PAD, LANES), jnp.bfloat16),
            pltpu.VMEM((n, arows, two), jnp.float32),
            pltpu.VMEM((n, zh, 2 * brows + PAD, LANES), jnp.bfloat16),
            pltpu.VMEM((n, zh - 1, 2 * brows + PAD, LANES), jnp.bfloat16),
            pltpu.VMEM((n, arows, two), jnp.float32),
            pltpu.VMEM((4, brows, two), jnp.float32),
            dma((3,)),
            dma((2, 2)), dma((2, 2)),
            dma((2, 2)), dma((2, 2)),
            dma((4, 2)), dma((4, 2)),
            dma((n, ny - 1)), dma((n, ny - 1)),
            dma((n, zl - 1)), dma((n, zl - 1)),
            dma((n, zh - 1)), dma((n, zh - 1)),
            pltpu.SemaphoreType.REGULAR, pltpu.SemaphoreType.REGULAR,
        ],
        compiler_params=pltpu.CompilerParams(
            collective_id=0, has_side_effects=True, vmem_limit_bytes=55104 * 1024),
        cost_estimate=pl.CostEstimate(
            flops=2 * tokens * feats * nx * 4 * width, bytes_accessed=2 * tokens * feats, transcendentals=0),
    )(activations, targets.T)
    return both[:brows], both[brows:]


def solution(mesh, sizes=(NX, NY, ZH, ZL)):
    return jax.shard_map(
        functools.partial(shards, sizes),
        mesh=mesh,
        in_specs=(P("tok", "feat"), P("tok", "feat")),
        out_specs=(P(("feat", "tok"), None), P(("feat", "tok"), None)),
        check_vma=False,
    )
```
